32 devices in a mesh: groups: 2 (over y), replica: 4 (over x, core), tensor: 4 (over z).
Axes of the slice: x: 2, y: 2, z: 4, core: 2. Of those that a mesh axis runs over, the one named last changes fastest.
Arguments:
- hidden: bfloat16 [2, 64, 16384], P(None, ('groups', 'replica'), 'tensor'), parts along dimension 1, may hold values from -6 to 6
- queries: bfloat16 [2, 64, 16384], P(None, ('groups', 'replica'), 'tensor'), parts along dimension 1, may hold values from -12 to 12
- stored_keys: bfloat16 [64, 256, 1024], P(('groups', 'replica'), 'tensor'), parts along dimension 0, may hold values from -6 to 6
- stored_values: bfloat16 [64, 256, 1024], P(('groups', 'replica'), 'tensor'), parts along dimension 0, may hold values from -6 to 6
- lengths: int32 [64], P(('groups', 'replica')), parts along dimension 0, may hold values from 128 to 256, as said below
- adapter_of_row: int32 [64], P(('groups', 'replica')), parts along dimension 0, may hold values from 0 to 15, as said below
- key_value_weight: bfloat16 [16384, 2048], P('tensor'), may hold values from -0.046875 to 0.046875
- adapter_down_weight: bfloat16 [16, 32, 16384], P('replica', None, 'tensor'), may hold values from -0.046875 to 0.046875
- adapter_up_weight: bfloat16 [16, 16, 2048], P('replica', None, 'tensor'), may hold values from -1.5 to 1.5
Outputs:
- attended: bfloat16 [2, 64, 16384], P(None, ('groups', 'replica'), 'tensor'), parts along dimension 1
- fresh_kv: bfloat16 [2, 64, 2048], P(None, ('groups', 'replica'), 'tensor'), parts along dimension 1
The draws below stay inside these ranges and needn't reach their ends.
There are 2 independent parts, one for each index of `groups`. The reference program is written for one: setup_inputs(seed, part) draws one part's arguments, and reference() takes and returns one part's arrays. A program takes and returns all parts, laid end to end along the dimension named above; an argument that names none is the same for every part. Nothing has to cross between parts.
Inputs may be any that keep to these rules, and one draw needn't show every extreme that they name: Row r's cache is valid at the positions below lengths[r]; some row has exactly 256. `adapter_of_row`: equal within every aligned block of 8 rows.
All inputs are finite; a program needn't handle non-finite values.
Results may differ from the reference program's by a relative error of at most 0.015.
Values may be sent and summed in bfloat16 or wider, within the bound.
A program may use at most 192 MiB of HBM per device.

```python
import math
import jax
import jax.numpy as jnp
from jax import lax

MODEL_WIDTH = 16384
QUERY_HEADS = 128
KEY_VALUE_HEADS = 8
HEAD_SIZE = 128
ADAPTER_RANK = 16
ADAPTER_COUNT = 16
DECODE_STEPS = 2
ROWS = 32
CACHE_LENGTH = 256
KEY_FEATURES = 1024
QD = 16384


def shared_signs(key):
    flips = jax.random.bernoulli(key, 0.5, (ROWS, HEAD_SIZE))
    return jnp.where(flips, 1.0, -1.0).astype(jnp.float32)


def chosen_rows():
    row_index = jnp.arange(ROWS)
    picked = row_index % 4 == 0
    target = (120.0 + 60.0 * (row_index // 4 % 3)).astype(jnp.float32)
    strength = target / (math.sqrt(HEAD_SIZE) * 6.0)
    return (picked, strength)


def draw_queries(key, part):
    signs = shared_signs(key)
    key = jax.random.fold_in(key, 3)
    values = 1.5 * jax.random.normal(key, (DECODE_STEPS, ROWS, QUERY_HEADS, HEAD_SIZE), jnp.float32)
    picked, strength = chosen_rows()
    aligned = strength[:, None] * signs
    head_index = jnp.arange(QUERY_HEADS)
    spots = picked[None, :, None, None] & (head_index == 0)[None, None, :, None]
    values = jnp.where(spots, aligned[None, :, None, :], values)
    values = jnp.clip(values, -12.0, 12.0)
    return values.reshape(DECODE_STEPS, ROWS, QUERY_HEADS * HEAD_SIZE).astype(jnp.bfloat16)


def draw_stored_keys(key, part):
    signs = shared_signs(key)
    key = jax.random.fold_in(key, 5)
    values = jnp.clip(jax.random.normal(key, (ROWS, CACHE_LENGTH, KEY_FEATURES), jnp.float32), -6.0, 6.0)
    picked, strength = chosen_rows()
    positions = jnp.arange(CACHE_LENGTH)
    columns = jnp.arange(KEY_FEATURES)
    first_spot = positions == CACHE_LENGTH // 8
    second_spot = positions == CACHE_LENGTH // 3
    level = jnp.where(first_spot, 6.0, 5.9375)
    padded_signs = jnp.pad(signs, ((0, 0), (0, KEY_FEATURES - HEAD_SIZE)))
    aligned = level[None, :, None] * padded_signs[:, None, :]
    spots = picked[:, None, None] & (first_spot | second_spot)[None, :, None] & (columns < HEAD_SIZE)[None, None, :]
    values = jnp.where(spots, aligned, values)
    return values.astype(jnp.bfloat16)


def draw_lengths(key, part):
    key = jax.random.fold_in(key, 7)
    draw_key, pick_key = jax.random.split(key)
    drawn = jax.random.randint(draw_key, (ROWS,), CACHE_LENGTH // 2, CACHE_LENGTH + 1)
    chosen = jax.random.randint(pick_key, (), 0, ROWS)
    return jnp.where(jnp.arange(ROWS) == chosen, CACHE_LENGTH, drawn).astype(jnp.int32)


def draw_adapter_of_row(key, part):
    key = jax.random.fold_in(key, 9)
    draw_key, pick_key = jax.random.split(key)
    block_count = ROWS // 8
    drawn = jax.random.randint(draw_key, (block_count,), 0, ADAPTER_COUNT)
    chosen = jax.random.randint(pick_key, (), 0, block_count)
    block_index = jnp.arange(block_count)
    drawn = jnp.where(block_index == chosen, ADAPTER_COUNT - 1, drawn)
    drawn = jnp.where(block_index == (chosen + 1) % block_count, 0, drawn)
    return jnp.repeat(drawn, 8).astype(jnp.int32)


def level_of(own_key, dims, cuts, least, largest):
    def one(axis_at, shards_of):
        steps = jax.random.uniform(jax.random.fold_in(jax.random.fold_in(own_key, 6), axis_at), (shards_of,), jnp.float32, least / len(cuts), largest / len(cuts))
        return jnp.repeat(jnp.exp(steps), dims[axis_at] // shards_of).reshape((-1,) + (1,) * (len(dims) - axis_at - 1))

    level = one(*cuts[0])
    for cut in cuts[1:]:
        level = level * one(*cut)
    return level


def normal_values(stream_key, dims, width, most, cuts=(), kind=jnp.bfloat16):
    values = jax.random.normal(stream_key, dims, jnp.float32) * width
    if len(cuts) > 0:
        values = level_of(stream_key, dims, cuts, -0.22, 0.18) * values
    return jnp.clip(values, min=-most, max=most).astype(kind)


def setup_inputs(seed: int = 0, part: int = 0) -> dict:
    arg_keys = jax.random.split(jax.random.key(seed), 10)
    own_keys = jax.random.split(jax.random.fold_in(arg_keys[9], part), 10)
    return {
        "hidden": normal_values(own_keys[0], (DECODE_STEPS, ROWS, MODEL_WIDTH), 1.0, 6.0, ((1, 4), (2, 4))),
        "queries": draw_queries(jax.random.fold_in(jax.random.fold_in(arg_keys[9], part), 71), part),
        "stored_keys": draw_stored_keys(jax.random.fold_in(jax.random.fold_in(arg_keys[9], part), 71), part),
        "stored_values": normal_values(own_keys[3], (ROWS, CACHE_LENGTH, KEY_FEATURES), 1.0, 6.0, ((0, 4), (1, 4))),
        "lengths": draw_lengths(jax.random.fold_in(jax.random.fold_in(arg_keys[9], part), 71), part),
        "adapter_of_row": draw_adapter_of_row(jax.random.fold_in(jax.random.fold_in(arg_keys[9], part), 71), part),
        "key_value_weight": normal_values(arg_keys[6], (MODEL_WIDTH, 2 * KEY_FEATURES), MODEL_WIDTH ** -0.5, 0.046875, ((0, 4),)),
        "adapter_down_weight": normal_values(arg_keys[7], (ADAPTER_COUNT, 2 * ADAPTER_RANK, MODEL_WIDTH), MODEL_WIDTH ** -0.5, 0.046875, ((0, 4), (2, 4))),
        "adapter_up_weight": normal_values(arg_keys[8], (ADAPTER_COUNT, ADAPTER_RANK, 2 * KEY_FEATURES), ADAPTER_RANK ** -0.5, 1.5, ((0, 4), (2, 4))),
    }


def reference(hidden, queries, stored_keys, stored_values, lengths, adapter_of_row, key_value_weight, adapter_down_weight, adapter_up_weight):
    hidden_broad = hidden.astype(jnp.float32)
    base_part = jnp.einsum('srd,dc->src', hidden_broad, key_value_weight.astype(jnp.float32))
    reduced_whole = jnp.einsum('qtc,mec->qtme', hidden_broad, adapter_down_weight.astype(jnp.float32))
    one_hot = (adapter_of_row[:, None] == jnp.arange(ADAPTER_COUNT)[None, :]).astype(jnp.float32)
    low_rank = lax.optimization_barrier(jnp.sum(reduced_whole * one_hot[None, :, :, None], axis=2))
    up_row_block = adapter_up_weight[adapter_of_row].astype(jnp.float32)
    key_delta = jnp.einsum('sri,ric->src', low_rank[..., :ADAPTER_RANK], up_row_block[..., :KEY_FEATURES], precision=lax.Precision.HIGHEST)
    value_delta = jnp.einsum('sri,ric->src', low_rank[..., ADAPTER_RANK:], up_row_block[..., KEY_FEATURES:], precision=lax.Precision.HIGHEST)
    fresh_kv = (base_part + jnp.concatenate([key_delta, value_delta], axis=-1)).astype(jnp.bfloat16)
    scale = 1.0 / math.sqrt(HEAD_SIZE)
    group_size = QUERY_HEADS // KEY_VALUE_HEADS

    def one_row(items):
        query_single_row, key_store_cache, value_store_cache, length, newest_row = items
        key_row_block = jnp.concatenate([key_store_cache, newest_row[:, :KEY_FEATURES]], axis=0).astype(jnp.float32).reshape(CACHE_LENGTH + DECODE_STEPS, KEY_VALUE_HEADS, HEAD_SIZE)
        value_row_block = jnp.concatenate([value_store_cache, newest_row[:, KEY_FEATURES:]], axis=0).astype(jnp.float32).reshape(CACHE_LENGTH + DECODE_STEPS, KEY_VALUE_HEADS, HEAD_SIZE)
        query_broad = query_single_row.astype(jnp.float32).reshape(DECODE_STEPS, KEY_VALUE_HEADS, group_size, HEAD_SIZE)
        scores = jnp.einsum('sgqd,pgd->sgqp', query_broad, key_row_block) * scale
        positions = jnp.arange(CACHE_LENGTH + DECODE_STEPS)
        step_index = jnp.arange(DECODE_STEPS)
        usable = jnp.where(positions[None, :] < CACHE_LENGTH, positions[None, :] < length, positions[None, :] - CACHE_LENGTH <= step_index[:, None])
        usable = usable[:, None, None, :]
        scores = jnp.where(usable, scores, -jnp.inf)
        row_top = lax.optimization_barrier(jnp.max(scores, axis=-1, keepdims=True))
        weights = jnp.where(usable, jnp.exp(scores - row_top), 0.0)
        totals = lax.optimization_barrier(jnp.sum(weights, axis=-1))
        rounded = lax.optimization_barrier(weights.astype(jnp.bfloat16)).astype(jnp.float32)
        summed = jnp.einsum('sgqp,pgd->sgqd', rounded, value_row_block)
        return (summed / totals[..., None]).reshape(DECODE_STEPS, QD).astype(jnp.bfloat16)
    attended = lax.map(one_row, (jnp.transpose(queries, (1, 0, 2)), stored_keys, stored_values, lengths, jnp.transpose(fresh_kv, (1, 0, 2))))
    return (jnp.transpose(attended, (1, 0, 2)), fresh_kv)
```

```python
import functools
import math

import jax
import jax.numpy as jnp
from jax import lax
from jax.experimental import pallas as pl
from jax.experimental.pallas import tpu as pltpu
from jax.sharding import PartitionSpec as P

QUERY_HEADS = 128
KEY_VALUE_HEADS = 8
HEAD_SIZE = 128


MASKED = -1e30


def joined(value, axis, join):
    pieces = jax.tree.map(lambda part: lax.all_gather(part, axis), value)
    head = jax.tree.map(lambda part: part[0], pieces)
    tail = jax.tree.map(lambda part: part[1:], pieces)
    total, _ = lax.scan(lambda total, piece: (join(total, piece), None), head, tail)
    return total


def combine_partial(earlier, later):
    first_top, first_total, first_acc = earlier
    second_top, second_total, second_acc = later
    joined_top = jnp.maximum(first_top, second_top)
    first_factor = jnp.exp(first_top - joined_top)
    second_factor = jnp.exp(second_top - joined_top)
    joined_total = first_total * first_factor + second_total * second_factor
    joined_acc = first_acc * first_factor[..., None] + second_acc * second_factor[..., None]
    return (joined_top, joined_total, joined_acc)


def per_device(
    hidden,
    queries,
    stored_keys,
    stored_values,
    lengths,
    adapter_of_row,
    key_value_weight,
    adapter_down_weight,
    adapter_up_weight,
):
    step_total, row_total, feat_count = hidden.shape
    kv_width = key_value_weight.shape[1]
    key_value_half = kv_width // 2
    column_total = adapter_up_weight.shape[2]
    rank_width = adapter_up_weight.shape[1]
    block_count = row_total // 8
    tensor_index = lax.axis_index("tensor")
    col_start = tensor_index * column_total
    scale = 1.0 / math.sqrt(HEAD_SIZE)
    group_size = QUERY_HEADS // KEY_VALUE_HEADS
    down_all, up_part = (
        lax.all_gather(adapter_down_weight, "replica", axis=0, tiled=True),
        lax.all_gather(adapter_up_weight, "replica", axis=0, tiled=True),
    )
    block_ids = adapter_of_row.reshape(block_count, 8)[:, 0]
    down_used = jnp.take(down_all, block_ids, axis=0)
    grouped = hidden.reshape(step_total, block_count, 8, feat_count)
    low_rank = jnp.einsum("sbrd,bjd->sbrj", grouped, down_used, preferred_element_type=jnp.float32)
    base_part = jnp.dot(
        hidden.reshape(step_total * row_total, feat_count),
        key_value_weight,
        preferred_element_type=jnp.float32,
    )
    base_part = base_part.reshape(step_total, row_total, kv_width)
    up_full = lax.all_gather(up_part, "tensor", axis=2, tiled=True)
    up_used = jnp.take(up_full, block_ids, axis=0).astype(jnp.float32)
    key_delta = jnp.einsum(
        "sbri,bic->sbrc",
        low_rank[..., :rank_width],
        up_used[..., :key_value_half],
        precision=lax.Precision.HIGHEST,
    )
    value_delta = jnp.einsum(
        "sbri,bic->sbrc",
        low_rank[..., rank_width:],
        up_used[..., key_value_half:],
        precision=lax.Precision.HIGHEST,
    )
    low_delta = jnp.concatenate([key_delta, value_delta], axis=-1).reshape(
        step_total, row_total, kv_width
    )
    summed = lax.psum((base_part + low_delta).astype(jnp.bfloat16), "tensor")
    fresh_own = lax.dynamic_slice_in_dim(summed, col_start, column_total, 2)
    query_complete = lax.all_gather(queries, "tensor", axis=2, tiled=True)
    column_span = stored_keys.shape[1]
    positions = tensor_index * column_span + jnp.arange(column_span)
    usable = (positions[None, :] < lengths[:, None])[None, :, None, None, :]
    query_group_rows = query_complete.reshape(
        step_total, row_total, KEY_VALUE_HEADS, group_size, HEAD_SIZE
    )
    key_store_cache = stored_keys.reshape(row_total, column_span, KEY_VALUE_HEADS, HEAD_SIZE)
    value_store_cache = stored_values.reshape(row_total, column_span, KEY_VALUE_HEADS, HEAD_SIZE)
    scores = (
        jnp.einsum(
            "srgqd,rpgd->srgqp",
            query_group_rows,
            key_store_cache,
            preferred_element_type=jnp.float32,
        )
        * scale
    )
    scores = jnp.where(usable, scores, MASKED)
    local_top = jnp.max(scores, axis=-1)
    weights = jnp.where(usable, jnp.exp(scores - local_top[..., None]), 0.0)
    local_total = jnp.sum(weights, axis=-1).reshape(step_total, row_total, QUERY_HEADS)
    local_acc = jnp.einsum(
        "srgqp,rpgd->srgqd",
        weights.astype(jnp.bfloat16),
        value_store_cache,
        preferred_element_type=jnp.float32,
    )
    local_acc = local_acc.reshape(step_total, row_total, QUERY_HEADS, HEAD_SIZE)
    local_top = local_top.reshape(step_total, row_total, QUERY_HEADS)
    heads_here = queries.shape[2] // HEAD_SIZE
    head_start = tensor_index * heads_here
    merged_top, merged_total, merged_acc = joined(
        (local_top, local_total, local_acc), "tensor", combine_partial
    )
    row_top = lax.dynamic_slice_in_dim(merged_top, head_start, heads_here, 2)
    totals = lax.dynamic_slice_in_dim(merged_total, head_start, heads_here, 2)
    weighted = lax.dynamic_slice_in_dim(merged_acc, head_start, heads_here, 2)
    kv_of_head = (head_start + jnp.arange(heads_here)) // group_size
    newest_keys = summed[..., :key_value_half].reshape(
        step_total, row_total, KEY_VALUE_HEADS, HEAD_SIZE
    )
    newest_values = summed[..., key_value_half:].reshape(
        step_total, row_total, KEY_VALUE_HEADS, HEAD_SIZE
    )
    head_keys = jnp.take(newest_keys, kv_of_head, axis=2)
    head_values = jnp.take(newest_values, kv_of_head, axis=2)
    query_own = queries.reshape(step_total, row_total, heads_here, HEAD_SIZE)
    own_scores = (
        jnp.einsum("srhd,jrhd->srhj", query_own, head_keys, preferred_element_type=jnp.float32)
        * scale
    )
    step_index = jnp.arange(step_total)
    causal = (step_index[None, :] <= step_index[:, None])[:, None, None, :]
    own_scores = jnp.where(causal, own_scores, MASKED)
    new_top = jnp.maximum(row_top, jnp.max(own_scores, axis=-1))
    old_factor = jnp.exp(row_top - new_top)
    own_weights = jnp.where(causal, jnp.exp(own_scores - new_top[..., None]), 0.0)
    totals = totals * old_factor + jnp.sum(own_weights, axis=-1)
    own_part = jnp.einsum(
        "srhj,jrhd->srhd",
        own_weights.astype(jnp.bfloat16),
        head_values,
        preferred_element_type=jnp.float32,
    )
    weighted = weighted * old_factor[..., None] + own_part
    attended = (
        (weighted / totals[..., None])
        .astype(jnp.bfloat16)
        .reshape(step_total, row_total, heads_here * HEAD_SIZE)
    )
    return (attended, fresh_own)


MESH = pl.DeviceIdType.MESH
GROUP = QUERY_HEADS // KEY_VALUE_HEADS
CHUNKS = 8


def fused_kernel(
    tensor_size,
    replica_size,
    row_total,
    lengths_ref,
    ids_ref,
    hidden_ref,
    query_ref,
    up_ref,
    key_hbm,
    value_hbm,
    down_hbm,
    weight_hbm,
    out_ref,
    fresh_ref,
    key_buf,
    value_buf,
    down_buf,
    weight_buf,
    query_in,
    hidden_in,
    ids_in,
    base_out,
    base_in,
    low_out,
    low_in,
    up_wide,
    delta_out,
    delta_in,
    fresh_all,
    acc_out,
    acc_in,
    lse_out,
    lse_in,
    local_sem,
    weight_sem,
    t_send,
    t_recv,
    r_send,
    r_recv,
):
    T, R = tensor_size, replica_size
    t = lax.axis_index("tensor")
    r = lax.axis_index("replica")
    tokens, feat = hidden_ref.shape
    steps = tokens // row_total
    columns = up_ref.shape[2]
    ranks = up_ref.shape[1]
    adapters = up_ref.shape[0]
    span = key_buf.shape[1]
    blocks = query_ref.shape[0] // (row_total * steps * GROUP)
    per_row = steps * GROUP
    per_block = row_total * per_row
    scale = 1.0 / math.sqrt(HEAD_SIZE)
    depth = feat // CHUNKS

    local = [
        pltpu.make_async_copy(down_hbm, down_buf, local_sem.at[0]),
        pltpu.make_async_copy(key_hbm, key_buf, local_sem.at[1]),
        pltpu.make_async_copy(value_hbm, value_buf, local_sem.at[2]),
    ]
    weights = [
        pltpu.make_async_copy(
            weight_hbm.at[pl.ds(c * depth, depth)],
            weight_buf.at[pl.ds(c * depth, depth)],
            weight_sem.at[c],
        )
        for c in range(CHUNKS)
    ]
    for copy in weights[:2] + local + weights[2:]:
        copy.start()

    def along_t(kind, k, src, dst, sign=1):
        return pltpu.make_async_remote_copy(
            src_ref=src,
            dst_ref=dst,
            send_sem=t_send.at[kind, k],
            recv_sem=t_recv.at[kind, k],
            device_id={"tensor": lax.rem(t + sign * k + T, T)},
            device_id_type=MESH,
        )

    def along_r(kind, k, src, dst):
        return pltpu.make_async_remote_copy(
            src_ref=src,
            dst_ref=dst,
            send_sem=r_send.at[kind, k],
            recv_sem=r_recv.at[kind, k],
            device_id={"replica": lax.rem(r + k, R)},
            device_id_type=MESH,
        )

    lane = lax.broadcasted_iota(jnp.int32, (row_total, 128), 1)
    sub = lax.broadcasted_iota(jnp.int32, (row_total, 128), 0)
    ids = jnp.zeros((row_total, 128), jnp.int32)
    for i in range(row_total):
        ids = jnp.where(sub == i, ids_ref[i], ids)
    ids_in[0] = ids

    barrier = pltpu.get_barrier_semaphore()
    for k in range(1, T):
        pl.semaphore_signal(
            barrier, inc=1, device_id={"tensor": lax.rem(t + k, T)}, device_id_type=MESH
        )
    for k in range(1, R):
        pl.semaphore_signal(
            barrier, inc=1, device_id={"replica": lax.rem(r + k, R)}, device_id_type=MESH
        )
    pl.semaphore_wait(barrier, T - 1 + R - 1)

    started = []

    def start(copy):
        copy.start()
        started.append(copy)
        return copy

    hidden_moves = [start(along_r(0, k, hidden_ref, hidden_in.at[k - 1])) for k in range(1, R)]
    query_moves = [start(along_t(0, k, query_ref, query_in.at[k - 1])) for k in range(1, T)]
    ids_moves = [start(along_r(1, k, ids_in.at[0], ids_in.at[k])) for k in range(1, R)]

    up_wide[...] = jnp.zeros_like(up_wide)
    half = (t * columns) // (T * columns // 2)
    for a in range(adapters):
        up_wide[a, pl.ds(pl.multiple_of(half * ranks, ranks), ranks), :] = up_ref[a]

    total = None
    for c in range(CHUNKS):
        weights[c].wait()
        part = jnp.dot(
            hidden_ref[:, c * depth : (c + 1) * depth],
            weight_buf[c * depth : (c + 1) * depth, :],
            preferred_element_type=jnp.float32,
        )
        total = part if total is None else total + part
    for u in range(T):
        base_out[u] = total[:, u * columns : (u + 1) * columns].astype(base_out.dtype)
    base_moves = [
        start(along_t(1, k, base_out.at[lax.rem(t + k, T)], base_in.at[k - 1]))
        for k in range(1, T)
    ]

    local[0].wait()
    contract = (((1,), (1,)), ((), ()))
    for k in range(R):
        if k > 0:
            hidden_moves[k - 1].wait_recv()
        tokens_here = hidden_ref[...] if k == 0 else hidden_in[k - 1]
        low_out[k] = lax.dot_general(
            tokens_here, down_buf[...], contract, preferred_element_type=jnp.float32
        )
    low_moves = [start(along_t(2, k, low_out, low_in.at[k - 1])) for k in range(1, T)]

    local[1].wait()
    local[2].wait()
    place = t * span + lax.broadcasted_iota(jnp.int32, (per_row, span), 1)
    lse_lane = lax.broadcasted_iota(jnp.int32, (per_row, 128), 1)

    def attend(owner, query, slot):
        lse = jnp.full((per_row, 128), MASKED, jnp.float32)
        for b in range(blocks):
            cols = pl.ds(pl.multiple_of((owner * blocks + b) * HEAD_SIZE, HEAD_SIZE), HEAD_SIZE)
            for i in range(row_total):
                first = b * per_block + i * per_row
                usable = place < lengths_ref[i]
                scores = scale * lax.dot_general(
                    query[first : first + per_row, :],
                    key_buf[i, :, cols],
                    contract,
                    preferred_element_type=jnp.float32,
                )
                scores = jnp.where(usable, scores, MASKED)
                top = jnp.max(scores, axis=1, keepdims=True)
                wide = jnp.where(usable, jnp.exp(scores - top), 0.0)
                whole = jnp.maximum(jnp.sum(wide, axis=1, keepdims=True), 1.0)
                acc = jnp.dot(
                    wide.astype(jnp.bfloat16),
                    value_buf[i, :, cols],
                    preferred_element_type=jnp.float32,
                )
                acc_out[slot, first : first + per_row, :] = (acc / whole).astype(jnp.bfloat16)
                lse = jnp.where(lse_lane == b * row_total + i, top + jnp.log(whole), lse)
        lse_out[slot] = lse

    acc_moves, lse_moves = [], []
    for k in range(1, T):
        query_moves[k - 1].wait_recv()
        attend(lax.rem(t - k + T, T), query_in.at[k - 1], k)
        acc_moves.append(start(along_t(3, k, acc_out.at[k], acc_in.at[k - 1], -1)))
        lse_moves.append(start(along_t(4, k, lse_out.at[k], lse_in.at[k - 1], -1)))

    for move in low_moves:
        move.wait_recv()
    for move in ids_moves:
        move.wait_recv()
    wide_up = up_wide[...].reshape(adapters * 2 * ranks, columns)
    for k in range(R):
        low = low_out[k]
        for j in range(T - 1):
            low = low + low_in[j, k]
        mine = ids_in[k] == r * adapters + lane // (2 * ranks)
        low = jnp.where(jnp.concatenate([mine] * steps, axis=0), low, 0.0)
        high = low.astype(jnp.bfloat16)
        rest = (low - high.astype(jnp.float32)).astype(jnp.bfloat16)
        delta_out[k] = jnp.dot(high, wide_up, preferred_element_type=jnp.float32) + jnp.dot(
            rest, wide_up, preferred_element_type=jnp.float32
        )
    delta_moves = []
    for k in range(1, R):
        delta_moves.append(
            start(
                pltpu.make_async_remote_copy(
                    src_ref=delta_out.at[k],
                    dst_ref=delta_in.at[k - 1],
                    send_sem=r_send.at[2, k],
                    recv_sem=r_recv.at[2, k],
                    device_id={"replica": lax.rem(r - k + R, R)},
                    device_id_type=MESH,
                )
            )
        )

    attend(t, query_ref, 0)

    fresh = base_out[t].astype(jnp.float32) + delta_out[0]
    for move in base_moves:
        move.wait_recv()
    for k in range(1, T):
        fresh = fresh + base_in[k - 1].astype(jnp.float32)
    for move in delta_moves:
        move.wait_recv()
    for k in range(1, R):
        fresh = fresh + delta_in[k - 1]
    fresh = fresh.astype(jnp.bfloat16)
    fresh_ref[...] = fresh
    fresh_all[t] = fresh
    fresh_moves = [
        start(along_t(5, k, fresh_all.at[t], fresh_all.at[t])) for k in range(1, T)
    ]
    for move in fresh_moves:
        move.wait_recv()
    for move in acc_moves + lse_moves:
        move.wait_recv()

    line = lax.broadcasted_iota(jnp.int32, (per_block, tokens), 0)
    spot = lax.broadcasted_iota(jnp.int32, (per_block, tokens), 1)
    seen = (line // per_row == spot % row_total) & (spot // row_total <= (line % per_row) // GROUP)
    for b in range(blocks):
        column = (t * blocks + b) * HEAD_SIZE
        holder, offset = column // columns, lax.rem(column, columns)
        cols = pl.ds(pl.multiple_of(offset, HEAD_SIZE), HEAD_SIZE)
        new_keys = fresh_all[holder, :, cols]
        new_values = fresh_all[T // 2 + holder, :, cols]
        rows = slice(b * per_block, (b + 1) * per_block)
        scores = scale * lax.dot_general(
            query_ref[rows, :], new_keys, contract, preferred_element_type=jnp.float32
        )
        scores = jnp.where(seen, scores, MASKED)
        top = jnp.max(scores, axis=1, keepdims=True)
        levels = []
        for k in range(T):
            held = lse_out[0] if k == 0 else lse_in[k - 1]
            levels.append(
                jnp.concatenate(
                    [
                        held[:, b * row_total + i : b * row_total + i + 1]
                        for i in range(row_total)
                    ],
                    axis=0,
                )
            )
            top = jnp.maximum(top, levels[-1])
        wide = jnp.where(seen, jnp.exp(scores - top), 0.0)
        whole = jnp.sum(wide, axis=1, keepdims=True)
        acc = jnp.dot(wide.astype(jnp.bfloat16), new_values, preferred_element_type=jnp.float32)
        for k in range(T):
            factor = jnp.exp(levels[k] - top)
            held = acc_out[0, rows, :] if k == 0 else acc_in[k - 1, rows, :]
            whole = whole + factor
            acc = acc + factor * held.astype(jnp.float32)
        out_ref[rows, :] = (acc / whole).astype(jnp.bfloat16)

    for copy in started:
        copy.wait_send()


def fused(
    tensor_size,
    replica_size,
    hidden,
    queries,
    stored_keys,
    stored_values,
    lengths,
    adapter_of_row,
    key_value_weight,
    adapter_down_weight,
    adapter_up_weight,
):
    T, R = tensor_size, replica_size
    step_total, row_total, feat = hidden.shape
    adapters, rank_pair, _ = adapter_down_weight.shape
    columns = adapter_up_weight.shape[2]
    tokens = step_total * row_total
    heads_here = queries.shape[2] // HEAD_SIZE
    blocks = heads_here // GROUP
    lines = tokens * heads_here
    per_row = step_total * GROUP
    arranged = (
        queries.reshape(step_total, row_total, blocks, GROUP, HEAD_SIZE)
        .transpose(2, 1, 0, 3, 4)
        .reshape(lines, HEAD_SIZE)
    )
    bf16, f32 = jnp.bfloat16, jnp.float32
    vmem = pl.BlockSpec(memory_space=pltpu.VMEM)
    smem = pl.BlockSpec(memory_space=pltpu.SMEM)
    hbm = pl.BlockSpec(memory_space=pl.ANY)
    attended, fresh = pl.pallas_call(
        functools.partial(fused_kernel, T, R, row_total),
        out_shape=(
            jax.ShapeDtypeStruct((lines, HEAD_SIZE), bf16),
            jax.ShapeDtypeStruct((tokens, columns), bf16),
        ),
        in_specs=[smem, smem, vmem, vmem, vmem, hbm, hbm, hbm, hbm],
        out_specs=(vmem, vmem),
        scratch_shapes=[
            pltpu.VMEM(stored_keys.shape, bf16),
            pltpu.VMEM(stored_values.shape, bf16),
            pltpu.VMEM((adapters * rank_pair, feat), bf16),
            pltpu.VMEM(key_value_weight.shape, bf16),
            pltpu.VMEM((T - 1, lines, HEAD_SIZE), bf16),
            pltpu.VMEM((R - 1, tokens, feat), bf16),
            pltpu.VMEM((R, row_total, 128), jnp.int32),
            pltpu.VMEM((T, tokens, columns), bf16),
            pltpu.VMEM((T - 1, tokens, columns), bf16),
            pltpu.VMEM((R, tokens, adapters * rank_pair), f32),
            pltpu.VMEM((T - 1, R, tokens, adapters * rank_pair), f32),
            pltpu.VMEM((adapters, rank_pair, columns), bf16),
            pltpu.VMEM((R, tokens, columns), f32),
            pltpu.VMEM((R - 1, tokens, columns), f32),
            pltpu.VMEM((T, tokens, columns), bf16),
            pltpu.VMEM((T, lines, HEAD_SIZE), bf16),
            pltpu.VMEM((T - 1, lines, HEAD_SIZE), bf16),
            pltpu.VMEM((T, per_row, 128), f32),
            pltpu.VMEM((T - 1, per_row, 128), f32),
            pltpu.SemaphoreType.DMA((3,)),
            pltpu.SemaphoreType.DMA((CHUNKS,)),
            pltpu.SemaphoreType.DMA((6, T)),
            pltpu.SemaphoreType.DMA((6, T)),
            pltpu.SemaphoreType.DMA((3, R)),
            pltpu.SemaphoreType.DMA((3, R)),
        ],
        compiler_params=pltpu.CompilerParams(
            collective_id=0, has_side_effects=True, vmem_limit_bytes=48 * 1024 * 1024
        ),
        name="fused",
    )(
        lengths,
        adapter_of_row,
        hidden.reshape(tokens, feat),
        arranged,
        adapter_up_weight,
        stored_keys,
        stored_values,
        adapter_down_weight.reshape(adapters * rank_pair, feat),
        key_value_weight,
    )
    attended = (
        attended.reshape(blocks, row_total, step_total, GROUP, HEAD_SIZE)
        .transpose(2, 1, 0, 3, 4)
        .reshape(step_total, row_total, heads_here * HEAD_SIZE)
    )
    return (attended, fresh.reshape(step_total, row_total, columns))


def fits(tensor_size, hidden, queries, stored_keys, key_value_weight, down, up):
    heads_here = queries.shape[2] // HEAD_SIZE
    columns = up.shape[2]
    pieces = (hidden, stored_keys, stored_keys, key_value_weight, down)
    return (
        hidden.shape[0] * hidden.shape[1] == 16
        and hidden.shape[1] == 8
        and heads_here % GROUP == 0
        and columns % HEAD_SIZE == 0
        and tensor_size % 2 == 0
        and down.shape[0] * down.shape[1] == 128
        and up.shape[1] % 16 == 0
        and hidden.shape[2] % (CHUNKS * 128) == 0
        and heads_here // GROUP * hidden.shape[1] <= 128
        and sum(2 * piece.size for piece in pieces) <= 24 * 1024 * 1024
    )


def dispatch(tensor_size, replica_size, *args):
    hidden, queries, stored_keys = args[:3]
    key_value_weight, down, up = args[6:]
    if fits(tensor_size, hidden, queries, stored_keys, key_value_weight, down, up):
        return fused(tensor_size, replica_size, *args)
    return per_device(*args)


def solution(mesh):
    placed = (
        P(None, ("groups", "replica"), "tensor"),
        P(None, ("groups", "replica"), "tensor"),
        P(("groups", "replica"), "tensor", None),
        P(("groups", "replica"), "tensor", None),
        P(("groups", "replica")),
        P(("groups", "replica")),
        P("tensor", None),
        P("replica", None, "tensor"),
        P("replica", None, "tensor"),
    )
    return jax.shard_map(
        functools.partial(dispatch, mesh.shape["tensor"], mesh.shape["replica"]),
        mesh=mesh,
        in_specs=placed,
        out_specs=(
            P(None, ("groups", "replica"), "tensor"),
            P(None, ("groups", "replica"), "tensor"),
        ),
        check_vma=False,
    )
```

```python
import functools
import math

import jax
import jax.numpy as jnp
from jax import lax
from jax.experimental import pallas as pl
from jax.experimental.pallas import tpu as pltpu
from jax.sharding import PartitionSpec as P

QUERY_HEADS = 128
KEY_VALUE_HEADS = 8
HEAD_SIZE = 128


MASKED = -1e30


def joined(value, axis, join):
    pieces = jax.tree.map(lambda part: lax.all_gather(part, axis), value)
    head = jax.tree.map(lambda part: part[0], pieces)
    tail = jax.tree.map(lambda part: part[1:], pieces)
    total, _ = lax.scan(lambda total, piece: (join(total, piece), None), head, tail)
    return total


def combine_partial(earlier, later):
    first_top, first_total, first_acc = earlier
    second_top, second_total, second_acc = later
    joined_top = jnp.maximum(first_top, second_top)
    first_factor = jnp.exp(first_top - joined_top)
    second_factor = jnp.exp(second_top - joined_top)
    joined_total = first_total * first_factor + second_total * second_factor
    joined_acc = first_acc * first_factor[..., None] + second_acc * second_factor[..., None]
    return (joined_top, joined_total, joined_acc)


def per_device(
    hidden,
    queries,
    stored_keys,
    stored_values,
    lengths,
    adapter_of_row,
    key_value_weight,
    adapter_down_weight,
    adapter_up_weight,
):
    step_total, row_total, feat_count = hidden.shape
    kv_width = key_value_weight.shape[1]
    key_value_half = kv_width // 2
    column_total = adapter_up_weight.shape[2]
    rank_width = adapter_up_weight.shape[1]
    block_count = row_total // 8
    tensor_index = lax.axis_index("tensor")
    col_start = tensor_index * column_total
    scale = 1.0 / math.sqrt(HEAD_SIZE)
    group_size = QUERY_HEADS // KEY_VALUE_HEADS
    down_all, up_part = (
        lax.all_gather(adapter_down_weight, "replica", axis=0, tiled=True),
        lax.all_gather(adapter_up_weight, "replica", axis=0, tiled=True),
    )
    block_ids = adapter_of_row.reshape(block_count, 8)[:, 0]
    down_used = jnp.take(down_all, block_ids, axis=0)
    grouped = hidden.reshape(step_total, block_count, 8, feat_count)
    low_rank = jnp.einsum("sbrd,bjd->sbrj", grouped, down_used, preferred_element_type=jnp.float32)
    base_part = jnp.dot(
        hidden.reshape(step_total * row_total, feat_count),
        key_value_weight,
        preferred_element_type=jnp.float32,
    )
    base_part = base_part.reshape(step_total, row_total, kv_width)
    up_full = lax.all_gather(up_part, "tensor", axis=2, tiled=True)
    up_used = jnp.take(up_full, block_ids, axis=0).astype(jnp.float32)
    key_delta = jnp.einsum(
        "sbri,bic->sbrc",
        low_rank[..., :rank_width],
        up_used[..., :key_value_half],
        precision=lax.Precision.HIGHEST,
    )
    value_delta = jnp.einsum(
        "sbri,bic->sbrc",
        low_rank[..., rank_width:],
        up_used[..., key_value_half:],
        precision=lax.Precision.HIGHEST,
    )
    low_delta = jnp.concatenate([key_delta, value_delta], axis=-1).reshape(
        step_total, row_total, kv_width
    )
    summed = lax.psum((base_part + low_delta).astype(jnp.bfloat16), "tensor")
    fresh_own = lax.dynamic_slice_in_dim(summed, col_start, column_total, 2)
    query_complete = lax.all_gather(queries, "tensor", axis=2, tiled=True)
    column_span = stored_keys.shape[1]
    positions = tensor_index * column_span + jnp.arange(column_span)
    usable = (positions[None, :] < lengths[:, None])[None, :, None, None, :]
    query_group_rows = query_complete.reshape(
        step_total, row_total, KEY_VALUE_HEADS, group_size, HEAD_SIZE
    )
    key_store_cache = stored_keys.reshape(row_total, column_span, KEY_VALUE_HEADS, HEAD_SIZE)
    value_store_cache = stored_values.reshape(row_total, column_span, KEY_VALUE_HEADS, HEAD_SIZE)
    scores = (
        jnp.einsum(
            "srgqd,rpgd->srgqp",
            query_group_rows,
            key_store_cache,
            preferred_element_type=jnp.float32,
        )
        * scale
    )
    scores = jnp.where(usable, scores, MASKED)
    local_top = jnp.max(scores, axis=-1)
    weights = jnp.where(usable, jnp.exp(scores - local_top[..., None]), 0.0)
    local_total = jnp.sum(weights, axis=-1).reshape(step_total, row_total, QUERY_HEADS)
    local_acc = jnp.einsum(
        "srgqp,rpgd->srgqd",
        weights.astype(jnp.bfloat16),
        value_store_cache,
        preferred_element_type=jnp.float32,
    )
    local_acc = local_acc.reshape(step_total, row_total, QUERY_HEADS, HEAD_SIZE)
    local_top = local_top.reshape(step_total, row_total, QUERY_HEADS)
    heads_here = queries.shape[2] // HEAD_SIZE
    head_start = tensor_index * heads_here
    merged_top, merged_total, merged_acc = joined(
        (local_top, local_total, local_acc), "tensor", combine_partial
    )
    row_top = lax.dynamic_slice_in_dim(merged_top, head_start, heads_here, 2)
    totals = lax.dynamic_slice_in_dim(merged_total, head_start, heads_here, 2)
    weighted = lax.dynamic_slice_in_dim(merged_acc, head_start, heads_here, 2)
    kv_of_head = (head_start + jnp.arange(heads_here)) // group_size
    newest_keys = summed[..., :key_value_half].reshape(
        step_total, row_total, KEY_VALUE_HEADS, HEAD_SIZE
    )
    newest_values = summed[..., key_value_half:].reshape(
        step_total, row_total, KEY_VALUE_HEADS, HEAD_SIZE
    )
    head_keys = jnp.take(newest_keys, kv_of_head, axis=2)
    head_values = jnp.take(newest_values, kv_of_head, axis=2)
    query_own = queries.reshape(step_total, row_total, heads_here, HEAD_SIZE)
    own_scores = (
        jnp.einsum("srhd,jrhd->srhj", query_own, head_keys, preferred_element_type=jnp.float32)
        * scale
    )
    step_index = jnp.arange(step_total)
    causal = (step_index[None, :] <= step_index[:, None])[:, None, None, :]
    own_scores = jnp.where(causal, own_scores, MASKED)
    new_top = jnp.maximum(row_top, jnp.max(own_scores, axis=-1))
    old_factor = jnp.exp(row_top - new_top)
    own_weights = jnp.where(causal, jnp.exp(own_scores - new_top[..., None]), 0.0)
    totals = totals * old_factor + jnp.sum(own_weights, axis=-1)
    own_part = jnp.einsum(
        "srhj,jrhd->srhd",
        own_weights.astype(jnp.bfloat16),
        head_values,
        preferred_element_type=jnp.float32,
    )
    weighted = weighted * old_factor[..., None] + own_part
    attended = (
        (weighted / totals[..., None])
        .astype(jnp.bfloat16)
        .reshape(step_total, row_total, heads_here * HEAD_SIZE)
    )
    return (attended, fresh_own)


MESH = pl.DeviceIdType.MESH
GROUP = QUERY_HEADS // KEY_VALUE_HEADS
CHUNKS = 8


def rows_at_once(row_total, span):
    batch = max(1, min(row_total, 256 // span))
    while row_total % batch:
        batch -= 1
    return batch


def folded(value, width):
    shift = width
    while shift < value.shape[1]:
        value = value + pltpu.roll(value, shift, axis=1)
        shift *= 2
    return value


def fused_kernel(
    tensor_size,
    replica_size,
    row_total,
    lengths_ref,
    ids_ref,
    hidden_hbm,
    query_ref,
    up_hbm,
    key_hbm,
    value_hbm,
    down_hbm,
    weight_hbm,
    out_ref,
    fresh_ref,
    hidden_ref,
    up_ref,
    bias,
    key_buf,
    value_buf,
    down_buf,
    weight_buf,
    query_in,
    hidden_in,
    ids_in,
    base_out,
    base_in,
    low_out,
    low_in,
    up_wide,
    delta_out,
    delta_in,
    fresh_all,
    acc_out,
    acc_in,
    lse_out,
    lse_in,
    local_sem,
    weight_sem,
    t_send,
    t_recv,
    r_send,
    r_recv,
):
    T, R = tensor_size, replica_size
    t = lax.axis_index("tensor")
    r = lax.axis_index("replica")
    tokens, feat = hidden_hbm.shape
    steps = tokens // row_total
    adapters, ranks, columns = up_hbm.shape
    span = key_buf.shape[1]
    blocks = query_ref.shape[0] // (row_total * steps * GROUP)
    per_row = steps * GROUP
    per_block = row_total * per_row
    scale = 1.0 / math.sqrt(HEAD_SIZE)
    depth = feat // CHUNKS

    local = [
        pltpu.make_async_copy(down_hbm, down_buf, local_sem.at[0]),
        pltpu.make_async_copy(key_hbm, key_buf, local_sem.at[1]),
        pltpu.make_async_copy(value_hbm, value_buf, local_sem.at[2]),
    ]
    small = [
        pltpu.make_async_copy(hidden_hbm, hidden_ref, local_sem.at[3]),
        pltpu.make_async_copy(up_hbm, up_ref, local_sem.at[4]),
    ]
    weights = [
        pltpu.make_async_copy(
            weight_hbm.at[pl.ds(c * depth, depth)],
            weight_buf.at[pl.ds(c * depth, depth)],
            weight_sem.at[c],
        )
        for c in range(CHUNKS)
    ]
    for copy in small + weights[:2] + local + weights[2:]:
        copy.start()

    def along_t(kind, k, src, dst, sign=1):
        return pltpu.make_async_remote_copy(
            src_ref=src,
            dst_ref=dst,
            send_sem=t_send.at[kind, k],
            recv_sem=t_recv.at[kind, k],
            device_id={"tensor": lax.rem(t + sign * k + T, T)},
            device_id_type=MESH,
        )

    def along_r(kind, k, src, dst):
        return pltpu.make_async_remote_copy(
            src_ref=src,
            dst_ref=dst,
            send_sem=r_send.at[kind, k],
            recv_sem=r_recv.at[kind, k],
            device_id={"replica": lax.rem(r + k, R)},
            device_id_type=MESH,
        )

    lane = lax.broadcasted_iota(jnp.int32, (row_total, 128), 1)
    sub = lax.broadcasted_iota(jnp.int32, (row_total, 128), 0)
    ids = jnp.zeros((row_total, 128), jnp.int32)
    for i in range(row_total):
        ids = jnp.where(sub == i, ids_ref[i], ids)
    ids_in[0] = ids

    barrier = pltpu.get_barrier_semaphore()
    for k in range(1, T):
        pl.semaphore_signal(
            barrier, inc=1, device_id={"tensor": lax.rem(t + k, T)}, device_id_type=MESH
        )
    for k in range(1, R):
        pl.semaphore_signal(
            barrier, inc=1, device_id={"replica": lax.rem(r + k, R)}, device_id_type=MESH
        )
    pl.semaphore_wait(barrier, T - 1 + R - 1)

    started = []

    def start(copy):
        copy.start()
        started.append(copy)
        return copy

    query_moves = [start(along_t(0, k, query_ref, query_in.at[k - 1])) for k in range(1, T)]
    small[0].wait()
    hidden_moves = [start(along_r(0, k, hidden_ref, hidden_in.at[k - 1])) for k in range(1, R)]
    ids_moves = [start(along_r(1, k, ids_in.at[0], ids_in.at[k])) for k in range(1, R)]

    up_wide[...] = jnp.zeros_like(up_wide)
    half = (t * columns) // (T * columns // 2)
    small[1].wait()
    for a in range(adapters):
        up_wide[a, pl.ds(pl.multiple_of(half * ranks, ranks), ranks), :] = up_ref[a]

    batch = rows_at_once(row_total, span)
    tall, broad = batch * per_row, batch * span
    line = lax.broadcasted_iota(jnp.int32, (tall, broad), 0) // per_row
    spot = lax.broadcasted_iota(jnp.int32, (tall, broad), 1)
    place = t * span + spot % span
    for n in range(row_total // batch):
        limit = jnp.zeros((tall, broad), jnp.int32)
        for i in range(batch):
            limit = jnp.where(line == i, lengths_ref[n * batch + i], limit)
        bias[n] = jnp.where((line == spot // span) & (place < limit), 0.0, MASKED)

    total = None
    for c in range(CHUNKS):
        weights[c].wait()
        part = jnp.dot(
            hidden_ref[:, c * depth : (c + 1) * depth],
            weight_buf[c * depth : (c + 1) * depth, :],
            preferred_element_type=jnp.float32,
        )
        total = part if total is None else total + part
    for u in range(T):
        base_out[u] = total[:, u * columns : (u + 1) * columns].astype(base_out.dtype)
    base_moves = [
        start(along_t(1, k, base_out.at[lax.rem(t + k, T)], base_in.at[k - 1]))
        for k in range(1, T)
    ]

    local[0].wait()
    contract = (((1,), (1,)), ((), ()))
    token_lane = lax.broadcasted_iota(jnp.int32, (tokens, 128), 1)
    pair = 2 * ranks
    low = jnp.zeros((tokens, 128), jnp.float32)
    for k in range(R):
        if k > 0:
            hidden_moves[k - 1].wait_recv()
            ids_moves[k - 1].wait_recv()
        tokens_here = hidden_ref[...] if k == 0 else hidden_in[k - 1]
        features = lax.dot_general(
            tokens_here, down_buf[...], contract, preferred_element_type=jnp.float32
        )
        mine = ids_in[k] == r * adapters + lane // pair
        features = jnp.where(jnp.concatenate([mine] * steps, axis=0), features, 0.0)
        low = jnp.where(token_lane // pair == k, folded(features, pair), low)
    low_out[...] = low
    low_moves = [start(along_t(2, k, low_out, low_in.at[k - 1])) for k in range(1, T)]

    local[1].wait()
    local[2].wait()
    lse_lane = lax.broadcasted_iota(jnp.int32, (per_row, 128), 1)
    count = blocks * row_total

    def attend(owner, query, slot):
        lse = jnp.full((per_row, 128), MASKED, jnp.float32)
        for b in range(blocks):
            cols = pl.ds(pl.multiple_of((owner * blocks + b) * HEAD_SIZE, HEAD_SIZE), HEAD_SIZE)
            for n in range(row_total // batch):
                first = b * per_block + n * tall
                some = pl.ds(n * batch, batch)
                scores = bias[n] + scale * lax.dot_general(
                    query[first : first + tall, :],
                    key_buf[some, :, cols].reshape(broad, HEAD_SIZE),
                    contract,
                    preferred_element_type=jnp.float32,
                )
                top = jnp.max(scores, axis=1, keepdims=True)
                wide = jnp.exp(scores - top)
                whole = jnp.sum(wide, axis=1, keepdims=True)
                acc = jnp.dot(
                    wide.astype(jnp.bfloat16),
                    value_buf[some, :, cols].reshape(broad, HEAD_SIZE),
                    preferred_element_type=jnp.float32,
                )
                acc_out[slot, first : first + tall, :] = (acc * (1.0 / whole)).astype(jnp.bfloat16)
                level = top + jnp.log(whole)
                for i in range(batch):
                    lse = jnp.where(
                        lse_lane == b * row_total + n * batch + i,
                        level[i * per_row : (i + 1) * per_row],
                        lse,
                    )
        slab = lse[:8]
        for v in range(1, per_row // 8):
            moved = pltpu.roll(lse[8 * v : 8 * v + 8], v * count, axis=1)
            slab = jnp.where(lane // count == v, moved, slab)
        lse_out[slot] = slab

    acc_moves, lse_moves = [], []
    for k in range(1, T):
        query_moves[k - 1].wait_recv()
        attend(lax.rem(t - k + T, T), query_in.at[k - 1], k)
        acc_moves.append(start(along_t(3, k, acc_out.at[k], acc_in.at[k - 1], -1)))
        lse_moves.append(start(along_t(4, k, lse_out.at[k], lse_in.at[k - 1], -1)))

    for move in low_moves:
        move.wait_recv()
    packed = low_out[...]
    for j in range(T - 1):
        packed = packed + low_in[j]
    wide_up = up_wide[...].reshape(adapters * 2 * ranks, columns)
    for k in range(R):
        low = folded(jnp.where(token_lane // pair == k, packed, 0.0), pair)
        mine = ids_in[k] == r * adapters + lane // pair
        low = jnp.where(jnp.concatenate([mine] * steps, axis=0), low, 0.0)
        high = low.astype(jnp.bfloat16)
        rest = (low - high.astype(jnp.float32)).astype(jnp.bfloat16)
        delta_out[k] = jnp.dot(high, wide_up, preferred_element_type=jnp.float32) + jnp.dot(
            rest, wide_up, preferred_element_type=jnp.float32
        )
    delta_moves = []
    for k in range(1, R):
        delta_moves.append(
            start(
                pltpu.make_async_remote_copy(
                    src_ref=delta_out.at[k],
                    dst_ref=delta_in.at[k - 1],
                    send_sem=r_send.at[2, k],
                    recv_sem=r_recv.at[2, k],
                    device_id={"replica": lax.rem(r - k + R, R)},
                    device_id_type=MESH,
                )
            )
        )

    attend(t, query_ref, 0)

    fresh = base_out[t].astype(jnp.float32) + delta_out[0]
    for move in base_moves:
        move.wait_recv()
    for k in range(1, T):
        fresh = fresh + base_in[k - 1].astype(jnp.float32)
    for move in delta_moves:
        move.wait_recv()
    for k in range(1, R):
        fresh = fresh + delta_in[k - 1]
    fresh = fresh.astype(jnp.bfloat16)
    fresh_ref[...] = fresh
    fresh_all[t] = fresh
    fresh_moves = [
        start(along_t(5, k, fresh_all.at[t], fresh_all.at[t])) for k in range(1, T)
    ]
    for move in fresh_moves:
        move.wait_recv()
    for move in acc_moves + lse_moves:
        move.wait_recv()

    line = lax.broadcasted_iota(jnp.int32, (per_block, tokens), 0)
    spot = lax.broadcasted_iota(jnp.int32, (per_block, tokens), 1)
    seen = (line // per_row == spot % row_total) & (spot // row_total <= (line % per_row) // GROUP)
    for b in range(blocks):
        column = (t * blocks + b) * HEAD_SIZE
        holder, offset = column // columns, lax.rem(column, columns)
        cols = pl.ds(pl.multiple_of(offset, HEAD_SIZE), HEAD_SIZE)
        new_keys = fresh_all[holder, :, cols]
        new_values = fresh_all[T // 2 + holder, :, cols]
        rows = slice(b * per_block, (b + 1) * per_block)
        scores = scale * lax.dot_general(
            query_ref[rows, :], new_keys, contract, preferred_element_type=jnp.float32
        )
        scores = jnp.where(seen, scores, MASKED)
        top = jnp.max(scores, axis=1, keepdims=True)
        levels = []
        for k in range(T):
            held = lse_out[0] if k == 0 else lse_in[k - 1]
            levels.append(
                jnp.concatenate(
                    [
                        held[:, v * count + b * row_total + i : v * count + b * row_total + i + 1]
                        for i in range(row_total)
                        for v in range(per_row // 8)
                    ],
                    axis=0,
                )
            )
            top = jnp.maximum(top, levels[-1])
        wide = jnp.where(seen, jnp.exp(scores - top), 0.0)
        whole = jnp.sum(wide, axis=1, keepdims=True)
        acc = jnp.dot(wide.astype(jnp.bfloat16), new_values, preferred_element_type=jnp.float32)
        for k in range(T):
            factor = jnp.exp(levels[k] - top)
            held = acc_out[0, rows, :] if k == 0 else acc_in[k - 1, rows, :]
            whole = whole + factor
            acc = acc + factor * held.astype(jnp.float32)
        out_ref[rows, :] = (acc / whole).astype(jnp.bfloat16)

    for copy in started:
        copy.wait_send()


def fused(
    tensor_size,
    replica_size,
    hidden,
    queries,
    stored_keys,
    stored_values,
    lengths,
    adapter_of_row,
    key_value_weight,
    adapter_down_weight,
    adapter_up_weight,
):
    T, R = tensor_size, replica_size
    step_total, row_total, feat = hidden.shape
    adapters, rank_pair, _ = adapter_down_weight.shape
    columns = adapter_up_weight.shape[2]
    tokens = step_total * row_total
    heads_here = queries.shape[2] // HEAD_SIZE
    blocks = heads_here // GROUP
    lines = tokens * heads_here
    per_row = step_total * GROUP
    span = stored_keys.shape[1]
    batch = rows_at_once(row_total, span)
    arranged = (
        queries.reshape(step_total, row_total, blocks, GROUP, HEAD_SIZE)
        .transpose(2, 1, 0, 3, 4)
        .reshape(lines, HEAD_SIZE)
    )
    bf16, f32 = jnp.bfloat16, jnp.float32
    vmem = pl.BlockSpec(memory_space=pltpu.VMEM)
    smem = pl.BlockSpec(memory_space=pltpu.SMEM)
    hbm = pl.BlockSpec(memory_space=pltpu.HBM)
    attended, fresh = pl.pallas_call(
        functools.partial(fused_kernel, T, R, row_total),
        out_shape=(
            jax.ShapeDtypeStruct((lines, HEAD_SIZE), bf16),
            jax.ShapeDtypeStruct((tokens, columns), bf16),
        ),
        in_specs=[smem, smem, hbm, vmem, hbm, hbm, hbm, hbm, hbm],
        out_specs=(vmem, vmem),
        scratch_shapes=[
            pltpu.VMEM((tokens, feat), bf16),
            pltpu.VMEM(adapter_up_weight.shape, bf16),
            pltpu.VMEM((row_total // batch, batch * per_row, batch * span), f32),
            pltpu.VMEM(stored_keys.shape, bf16),
            pltpu.VMEM(stored_values.shape, bf16),
            pltpu.VMEM((adapters * rank_pair, feat), bf16),
            pltpu.VMEM(key_value_weight.shape, bf16),
            pltpu.VMEM((T - 1, lines, HEAD_SIZE), bf16),
            pltpu.VMEM((R - 1, tokens, feat), bf16),
            pltpu.VMEM((R, row_total, 128), jnp.int32),
            pltpu.VMEM((T, tokens, columns), bf16),
            pltpu.VMEM((T - 1, tokens, columns), bf16),
            pltpu.VMEM((tokens, 128), f32),
            pltpu.VMEM((T - 1, tokens, 128), f32),
            pltpu.VMEM((adapters, rank_pair, columns), bf16),
            pltpu.VMEM((R, tokens, columns), f32),
            pltpu.VMEM((R - 1, tokens, columns), f32),
            pltpu.VMEM((T, tokens, columns), bf16),
            pltpu.VMEM((T, lines, HEAD_SIZE), bf16),
            pltpu.VMEM((T - 1, lines, HEAD_SIZE), bf16),
            pltpu.VMEM((T, 8, 128), f32),
            pltpu.VMEM((T - 1, 8, 128), f32),
            pltpu.SemaphoreType.DMA((5,)),
            pltpu.SemaphoreType.DMA((CHUNKS,)),
            pltpu.SemaphoreType.DMA((6, T)),
            pltpu.SemaphoreType.DMA((6, T)),
            pltpu.SemaphoreType.DMA((3, R)),
            pltpu.SemaphoreType.DMA((3, R)),
        ],
        compiler_params=pltpu.CompilerParams(
            collective_id=0, has_side_effects=True, vmem_limit_bytes=48 * 1024 * 1024
        ),
        name="fused",
    )(
        lengths,
        adapter_of_row,
        hidden.reshape(tokens, feat),
        arranged,
        adapter_up_weight,
        stored_keys,
        stored_values,
        adapter_down_weight.reshape(adapters * rank_pair, feat),
        key_value_weight,
    )
    attended = (
        attended.reshape(blocks, row_total, step_total, GROUP, HEAD_SIZE)
        .transpose(2, 1, 0, 3, 4)
        .reshape(step_total, row_total, heads_here * HEAD_SIZE)
    )
    return (attended, fresh.reshape(step_total, row_total, columns))


def fits(tensor_size, replica_size, hidden, queries, stored_keys, key_value_weight, down, up):
    heads_here = queries.shape[2] // HEAD_SIZE
    columns = up.shape[2]
    pieces = (hidden, stored_keys, stored_keys, key_value_weight, down)
    return (
        hidden.shape[0] * hidden.shape[1] == 16
        and hidden.shape[1] == 8
        and heads_here % GROUP == 0
        and columns % HEAD_SIZE == 0
        and tensor_size % 2 == 0
        and down.shape[0] * down.shape[1] == 128
        and replica_size * down.shape[1] <= 128
        and up.shape[1] % 16 == 0
        and hidden.shape[2] % (CHUNKS * 128) == 0
        and heads_here // GROUP * hidden.shape[1] * hidden.shape[0] * GROUP <= 1024
        and 256 % stored_keys.shape[1] == 0
        and sum(2 * piece.size for piece in pieces) <= 24 * 1024 * 1024
    )


def dispatch(tensor_size, replica_size, *args):
    hidden, queries, stored_keys = args[:3]
    key_value_weight, down, up = args[6:]
    if fits(tensor_size, replica_size, hidden, queries, stored_keys, key_value_weight, down, up):
        return fused(tensor_size, replica_size, *args)
    return per_device(*args)


def solution(mesh):
    placed = (
        P(None, ("groups", "replica"), "tensor"),
        P(None, ("groups", "replica"), "tensor"),
        P(("groups", "replica"), "tensor", None),
        P(("groups", "replica"), "tensor", None),
        P(("groups", "replica")),
        P(("groups", "replica")),
        P("tensor", None),
        P("replica", None, "tensor"),
        P("replica", None, "tensor"),
    )
    return jax.shard_map(
        functools.partial(dispatch, mesh.shape["tensor"], mesh.shape["replica"]),
        mesh=mesh,
        in_specs=placed,
        out_specs=(
            P(None, ("groups", "replica"), "tensor"),
            P(None, ("groups", "replica"), "tensor"),
        ),
        check_vma=False,
    )
```

```python
import functools
import math

import jax
import jax.numpy as jnp
from jax import lax
from jax.experimental import pallas as pl
from jax.experimental.pallas import tpu as pltpu
from jax.sharding import PartitionSpec as P

QUERY_HEADS = 128
KEY_VALUE_HEADS = 8
HEAD_SIZE = 128


MASKED = -1e30


def joined(value, axis, join):
    pieces = jax.tree.map(lambda part: lax.all_gather(part, axis), value)
    head = jax.tree.map(lambda part: part[0], pieces)
    tail = jax.tree.map(lambda part: part[1:], pieces)
    total, _ = lax.scan(lambda total, piece: (join(total, piece), None), head, tail)
    return total


def combine_partial(earlier, later):
    first_top, first_total, first_acc = earlier
    second_top, second_total, second_acc = later
    joined_top = jnp.maximum(first_top, second_top)
    first_factor = jnp.exp(first_top - joined_top)
    second_factor = jnp.exp(second_top - joined_top)
    joined_total = first_total * first_factor + second_total * second_factor
    joined_acc = first_acc * first_factor[..., None] + second_acc * second_factor[..., None]
    return (joined_top, joined_total, joined_acc)


def per_device(
    hidden,
    queries,
    stored_keys,
    stored_values,
    lengths,
    adapter_of_row,
    key_value_weight,
    adapter_down_weight,
    adapter_up_weight,
):
    step_total, row_total, feat_count = hidden.shape
    kv_width = key_value_weight.shape[1]
    key_value_half = kv_width // 2
    column_total = adapter_up_weight.shape[2]
    rank_width = adapter_up_weight.shape[1]
    block_count = row_total // 8
    tensor_index = lax.axis_index("tensor")
    col_start = tensor_index * column_total
    scale = 1.0 / math.sqrt(HEAD_SIZE)
    group_size = QUERY_HEADS // KEY_VALUE_HEADS
    down_all, up_part = (
        lax.all_gather(adapter_down_weight, "replica", axis=0, tiled=True),
        lax.all_gather(adapter_up_weight, "replica", axis=0, tiled=True),
    )
    block_ids = adapter_of_row.reshape(block_count, 8)[:, 0]
    down_used = jnp.take(down_all, block_ids, axis=0)
    grouped = hidden.reshape(step_total, block_count, 8, feat_count)
    low_rank = jnp.einsum("sbrd,bjd->sbrj", grouped, down_used, preferred_element_type=jnp.float32)
    base_part = jnp.dot(
        hidden.reshape(step_total * row_total, feat_count),
        key_value_weight,
        preferred_element_type=jnp.float32,
    )
    base_part = base_part.reshape(step_total, row_total, kv_width)
    up_full = lax.all_gather(up_part, "tensor", axis=2, tiled=True)
    up_used = jnp.take(up_full, block_ids, axis=0).astype(jnp.float32)
    key_delta = jnp.einsum(
        "sbri,bic->sbrc",
        low_rank[..., :rank_width],
        up_used[..., :key_value_half],
        precision=lax.Precision.HIGHEST,
    )
    value_delta = jnp.einsum(
        "sbri,bic->sbrc",
        low_rank[..., rank_width:],
        up_used[..., key_value_half:],
        precision=lax.Precision.HIGHEST,
    )
    low_delta = jnp.concatenate([key_delta, value_delta], axis=-1).reshape(
        step_total, row_total, kv_width
    )
    summed = lax.psum((base_part + low_delta).astype(jnp.bfloat16), "tensor")
    fresh_own = lax.dynamic_slice_in_dim(summed, col_start, column_total, 2)
    query_complete = lax.all_gather(queries, "tensor", axis=2, tiled=True)
    column_span = stored_keys.shape[1]
    positions = tensor_index * column_span + jnp.arange(column_span)
    usable = (positions[None, :] < lengths[:, None])[None, :, None, None, :]
    query_group_rows = query_complete.reshape(
        step_total, row_total, KEY_VALUE_HEADS, group_size, HEAD_SIZE
    )
    key_store_cache = stored_keys.reshape(row_total, column_span, KEY_VALUE_HEADS, HEAD_SIZE)
    value_store_cache = stored_values.reshape(row_total, column_span, KEY_VALUE_HEADS, HEAD_SIZE)
    scores = (
        jnp.einsum(
            "srgqd,rpgd->srgqp",
            query_group_rows,
            key_store_cache,
            preferred_element_type=jnp.float32,
        )
        * scale
    )
    scores = jnp.where(usable, scores, MASKED)
    local_top = jnp.max(scores, axis=-1)
    weights = jnp.where(usable, jnp.exp(scores - local_top[..., None]), 0.0)
    local_total = jnp.sum(weights, axis=-1).reshape(step_total, row_total, QUERY_HEADS)
    local_acc = jnp.einsum(
        "srgqp,rpgd->srgqd",
        weights.astype(jnp.bfloat16),
        value_store_cache,
        preferred_element_type=jnp.float32,
    )
    local_acc = local_acc.reshape(step_total, row_total, QUERY_HEADS, HEAD_SIZE)
    local_top = local_top.reshape(step_total, row_total, QUERY_HEADS)
    heads_here = queries.shape[2] // HEAD_SIZE
    head_start = tensor_index * heads_here
    merged_top, merged_total, merged_acc = joined(
        (local_top, local_total, local_acc), "tensor", combine_partial
    )
    row_top = lax.dynamic_slice_in_dim(merged_top, head_start, heads_here, 2)
    totals = lax.dynamic_slice_in_dim(merged_total, head_start, heads_here, 2)
    weighted = lax.dynamic_slice_in_dim(merged_acc, head_start, heads_here, 2)
    kv_of_head = (head_start + jnp.arange(heads_here)) // group_size
    newest_keys = summed[..., :key_value_half].reshape(
        step_total, row_total, KEY_VALUE_HEADS, HEAD_SIZE
    )
    newest_values = summed[..., key_value_half:].reshape(
        step_total, row_total, KEY_VALUE_HEADS, HEAD_SIZE
    )
    head_keys = jnp.take(newest_keys, kv_of_head, axis=2)
    head_values = jnp.take(newest_values, kv_of_head, axis=2)
    query_own = queries.reshape(step_total, row_total, heads_here, HEAD_SIZE)
    own_scores = (
        jnp.einsum("srhd,jrhd->srhj", query_own, head_keys, preferred_element_type=jnp.float32)
        * scale
    )
    step_index = jnp.arange(step_total)
    causal = (step_index[None, :] <= step_index[:, None])[:, None, None, :]
    own_scores = jnp.where(causal, own_scores, MASKED)
    new_top = jnp.maximum(row_top, jnp.max(own_scores, axis=-1))
    old_factor = jnp.exp(row_top - new_top)
    own_weights = jnp.where(causal, jnp.exp(own_scores - new_top[..., None]), 0.0)
    totals = totals * old_factor + jnp.sum(own_weights, axis=-1)
    own_part = jnp.einsum(
        "srhj,jrhd->srhd",
        own_weights.astype(jnp.bfloat16),
        head_values,
        preferred_element_type=jnp.float32,
    )
    weighted = weighted * old_factor[..., None] + own_part
    attended = (
        (weighted / totals[..., None])
        .astype(jnp.bfloat16)
        .reshape(step_total, row_total, heads_here * HEAD_SIZE)
    )
    return (attended, fresh_own)


MESH = pl.DeviceIdType.MESH
GROUP = QUERY_HEADS // KEY_VALUE_HEADS
CHUNKS = 8


def rows_at_once(row_total, span):
    batch = max(1, min(row_total, 256 // span))
    while row_total % batch:
        batch -= 1
    return batch


def folded(value, width):
    shift = width
    while shift < value.shape[1]:
        value = value + pltpu.roll(value, shift, axis=1)
        shift *= 2
    return value


def fused_kernel(
    tensor_size,
    replica_size,
    row_total,
    lengths_ref,
    ids_ref,
    hidden_hbm,
    query_ref,
    up_hbm,
    key_hbm,
    value_hbm,
    down_hbm,
    weight_hbm,
    out_ref,
    fresh_ref,
    hidden_ref,
    up_ref,
    bias,
    key_buf,
    value_buf,
    down_buf,
    weight_buf,
    query_in,
    hidden_in,
    ids_in,
    base_out,
    base_in,
    low_out,
    low_in,
    up_wide,
    delta_out,
    delta_in,
    fresh_all,
    acc_out,
    acc_in,
    lse_out,
    lse_in,
    local_sem,
    weight_sem,
    t_send,
    t_recv,
    r_send,
    r_recv,
):
    T, R = tensor_size, replica_size
    t = lax.axis_index("tensor")
    r = lax.axis_index("replica")
    tokens, feat = hidden_hbm.shape
    steps = tokens // row_total
    adapters, ranks, columns = up_hbm.shape
    span = key_buf.shape[1]
    blocks = query_ref.shape[0] // (row_total * steps * GROUP)
    per_row = steps * GROUP
    per_block = row_total * per_row
    scale = 1.0 / math.sqrt(HEAD_SIZE)
    depth = feat // CHUNKS

    local = [
        pltpu.make_async_copy(down_hbm, down_buf, local_sem.at[0]),
        pltpu.make_async_copy(key_hbm, key_buf, local_sem.at[1]),
        pltpu.make_async_copy(value_hbm, value_buf, local_sem.at[2]),
    ]
    small = [
        pltpu.make_async_copy(hidden_hbm, hidden_ref, local_sem.at[3]),
        pltpu.make_async_copy(up_hbm, up_ref, local_sem.at[4]),
    ]
    weights = [
        pltpu.make_async_copy(
            weight_hbm.at[pl.ds(c * depth, depth)],
            weight_buf.at[pl.ds(c * depth, depth)],
            weight_sem.at[c],
        )
        for c in range(CHUNKS)
    ]
    for copy in small + weights[:2] + local + weights[2:]:
        copy.start()

    def along_t(kind, k, src, dst, sign=1):
        return pltpu.make_async_remote_copy(
            src_ref=src,
            dst_ref=dst,
            send_sem=t_send.at[kind, k],
            recv_sem=t_recv.at[kind, k],
            device_id={"tensor": lax.rem(t + sign * k + T, T)},
            device_id_type=MESH,
        )

    def along_r(kind, k, src, dst):
        return pltpu.make_async_remote_copy(
            src_ref=src,
            dst_ref=dst,
            send_sem=r_send.at[kind, k],
            recv_sem=r_recv.at[kind, k],
            device_id={"replica": lax.rem(r + k, R)},
            device_id_type=MESH,
        )

    lane = lax.broadcasted_iota(jnp.int32, (row_total, 128), 1)
    sub = lax.broadcasted_iota(jnp.int32, (row_total, 128), 0)
    ids = jnp.zeros((row_total, 128), jnp.int32)
    for i in range(row_total):
        ids = jnp.where(sub == i, ids_ref[i], ids)
    ids_in[0] = ids

    barrier = pltpu.get_barrier_semaphore()
    for k in range(1, T):
        pl.semaphore_signal(
            barrier, inc=1, device_id={"tensor": lax.rem(t + k, T)}, device_id_type=MESH
        )
    for k in range(1, R):
        pl.semaphore_signal(
            barrier, inc=1, device_id={"replica": lax.rem(r + k, R)}, device_id_type=MESH
        )
    pl.semaphore_wait(barrier, T - 1 + R - 1)

    started = []

    def start(copy):
        copy.start()
        started.append(copy)
        return copy

    parts = [pl.ds(b * per_block, per_block) for b in range(blocks)]
    query_moves = [
        [
            start(along_t(6 + b, k, query_ref.at[parts[b]], query_in.at[k - 1, parts[b]]))
            for k in range(1, T)
        ]
        for b in range(blocks)
    ]
    small[0].wait()
    hidden_moves = [start(along_r(0, k, hidden_ref, hidden_in.at[k - 1])) for k in range(1, R)]
    ids_moves = [start(along_r(1, k, ids_in.at[0], ids_in.at[k])) for k in range(1, R)]

    up_wide[...] = jnp.zeros_like(up_wide)
    half = (t * columns) // (T * columns // 2)
    small[1].wait()
    for a in range(adapters):
        up_wide[a, pl.ds(pl.multiple_of(half * ranks, ranks), ranks), :] = up_ref[a]

    batch = rows_at_once(row_total, span)
    tall, broad = batch * per_row, batch * span
    line = lax.broadcasted_iota(jnp.int32, (tall, broad), 0) // per_row
    spot = lax.broadcasted_iota(jnp.int32, (tall, broad), 1)
    place = t * span + spot % span
    for n in range(row_total // batch):
        limit = jnp.zeros((tall, broad), jnp.int32)
        for i in range(batch):
            limit = jnp.where(line == i, lengths_ref[n * batch + i], limit)
        bias[n] = jnp.where((line == spot // span) & (place < limit), 0.0, MASKED)

    total = None
    for c in range(CHUNKS):
        weights[c].wait()
        part = jnp.dot(
            hidden_ref[:, c * depth : (c + 1) * depth],
            weight_buf[c * depth : (c + 1) * depth, :],
            preferred_element_type=jnp.float32,
        )
        total = part if total is None else total + part
    for u in range(T):
        base_out[u] = total[:, u * columns : (u + 1) * columns].astype(base_out.dtype)
    base_moves = [
        start(along_t(1, k, base_out.at[lax.rem(t + k, T)], base_in.at[k - 1]))
        for k in range(1, T)
    ]

    local[0].wait()
    contract = (((1,), (1,)), ((), ()))
    token_lane = lax.broadcasted_iota(jnp.int32, (tokens, 128), 1)
    pair = 2 * ranks
    low = jnp.zeros((tokens, 128), jnp.float32)
    for k in range(R):
        if k > 0:
            hidden_moves[k - 1].wait_recv()
            ids_moves[k - 1].wait_recv()
        tokens_here = hidden_ref[...] if k == 0 else hidden_in[k - 1]
        features = lax.dot_general(
            tokens_here, down_buf[...], contract, preferred_element_type=jnp.float32
        )
        mine = ids_in[k] == r * adapters + lane // pair
        features = jnp.where(jnp.concatenate([mine] * steps, axis=0), features, 0.0)
        low = jnp.where(token_lane // pair == k, folded(features, pair), low)
    low_out[...] = low
    low_moves = [start(along_t(2, k, low_out, low_in.at[k - 1])) for k in range(1, T)]

    local[1].wait()
    local[2].wait()
    lse_lane = lax.broadcasted_iota(jnp.int32, (per_row, 128), 1)
    count = blocks * row_total

    def attend(owner, query, slot, b, lse):
        cols = pl.ds(pl.multiple_of((owner * blocks + b) * HEAD_SIZE, HEAD_SIZE), HEAD_SIZE)
        for n in range(row_total // batch):
            first = b * per_block + n * tall
            some = pl.ds(n * batch, batch)
            scores = bias[n] + scale * lax.dot_general(
                query[first : first + tall, :],
                key_buf[some, :, cols].reshape(broad, HEAD_SIZE),
                contract,
                preferred_element_type=jnp.float32,
            )
            top = jnp.max(scores, axis=1, keepdims=True)
            wide = jnp.exp(scores - top)
            whole = jnp.sum(wide, axis=1, keepdims=True)
            acc = jnp.dot(
                wide.astype(jnp.bfloat16),
                value_buf[some, :, cols].reshape(broad, HEAD_SIZE),
                preferred_element_type=jnp.float32,
            )
            acc_out[slot, first : first + tall, :] = (acc * (1.0 / whole)).astype(jnp.bfloat16)
            level = top + jnp.log(whole)
            for i in range(batch):
                lse = jnp.where(
                    lse_lane == b * row_total + n * batch + i,
                    level[i * per_row : (i + 1) * per_row],
                    lse,
                )
        return lse

    def pack(lse, slot):
        slab = lse[:8]
        for v in range(1, per_row // 8):
            moved = pltpu.roll(lse[8 * v : 8 * v + 8], v * count, axis=1)
            slab = jnp.where(lane // count == v, moved, slab)
        lse_out[slot] = slab

    levels_of = [jnp.full((per_row, 128), MASKED, jnp.float32)] * T
    acc_moves, lse_moves = [[] for _ in range(blocks)], []

    def attend_remote(b):
        for k in range(1, T):
            query_moves[b][k - 1].wait_recv()
            owner = lax.rem(t - k + T, T)
            levels_of[k] = attend(owner, query_in.at[k - 1], k, b, levels_of[k])
            source, target = acc_out.at[k, parts[b]], acc_in.at[k - 1, parts[b]]
            acc_moves[b].append(start(along_t(6 + blocks + b, k, source, target, -1)))
            if b == blocks - 1:
                pack(levels_of[k], k)
                lse_moves.append(start(along_t(4, k, lse_out.at[k], lse_in.at[k - 1], -1)))

    for b in range(blocks - 1):
        attend_remote(b)

    for move in low_moves:
        move.wait_recv()
    packed = low_out[...]
    for j in range(T - 1):
        packed = packed + low_in[j]
    wide_up = up_wide[...].reshape(adapters * 2 * ranks, columns)
    for k in range(R):
        low = folded(jnp.where(token_lane // pair == k, packed, 0.0), pair)
        mine = ids_in[k] == r * adapters + lane // pair
        low = jnp.where(jnp.concatenate([mine] * steps, axis=0), low, 0.0)
        high = low.astype(jnp.bfloat16)
        rest = (low - high.astype(jnp.float32)).astype(jnp.bfloat16)
        delta_out[k] = jnp.dot(high, wide_up, preferred_element_type=jnp.float32) + jnp.dot(
            rest, wide_up, preferred_element_type=jnp.float32
        )
    delta_moves = []
    for k in range(1, R):
        delta_moves.append(
            start(
                pltpu.make_async_remote_copy(
                    src_ref=delta_out.at[k],
                    dst_ref=delta_in.at[k - 1],
                    send_sem=r_send.at[2, k],
                    recv_sem=r_recv.at[2, k],
                    device_id={"replica": lax.rem(r - k + R, R)},
                    device_id_type=MESH,
                )
            )
        )

    attend_remote(blocks - 1)

    fresh = base_out[t].astype(jnp.float32) + delta_out[0]
    for move in base_moves:
        move.wait_recv()
    for k in range(1, T):
        fresh = fresh + base_in[k - 1].astype(jnp.float32)
    for move in delta_moves:
        move.wait_recv()
    for k in range(1, R):
        fresh = fresh + delta_in[k - 1]
    fresh = fresh.astype(jnp.bfloat16)
    fresh_ref[...] = fresh
    fresh_all[t] = fresh
    fresh_moves = [
        start(along_t(5, k, fresh_all.at[t], fresh_all.at[t])) for k in range(1, T)
    ]
    for b in range(blocks):
        levels_of[0] = attend(t, query_ref, 0, b, levels_of[0])
    pack(levels_of[0], 0)

    for move in fresh_moves + lse_moves:
        move.wait_recv()

    line = lax.broadcasted_iota(jnp.int32, (per_block, tokens), 0)
    spot = lax.broadcasted_iota(jnp.int32, (per_block, tokens), 1)
    seen = (line // per_row == spot % row_total) & (spot // row_total <= (line % per_row) // GROUP)
    for b in range(blocks):
        for move in acc_moves[b]:
            move.wait_recv()
        column = (t * blocks + b) * HEAD_SIZE
        holder, offset = column // columns, lax.rem(column, columns)
        cols = pl.ds(pl.multiple_of(offset, HEAD_SIZE), HEAD_SIZE)
        new_keys = fresh_all[holder, :, cols]
        new_values = fresh_all[T // 2 + holder, :, cols]
        rows = slice(b * per_block, (b + 1) * per_block)
        scores = scale * lax.dot_general(
            query_ref[rows, :], new_keys, contract, preferred_element_type=jnp.float32
        )
        scores = jnp.where(seen, scores, MASKED)
        top = jnp.max(scores, axis=1, keepdims=True)
        levels = []
        for k in range(T):
            held = lse_out[0] if k == 0 else lse_in[k - 1]
            levels.append(
                jnp.concatenate(
                    [
                        held[:, v * count + b * row_total + i : v * count + b * row_total + i + 1]
                        for i in range(row_total)
                        for v in range(per_row // 8)
                    ],
                    axis=0,
                )
            )
            top = jnp.maximum(top, levels[-1])
        wide = jnp.where(seen, jnp.exp(scores - top), 0.0)
        whole = jnp.sum(wide, axis=1, keepdims=True)
        acc = jnp.dot(wide.astype(jnp.bfloat16), new_values, preferred_element_type=jnp.float32)
        for k in range(T):
            factor = jnp.exp(levels[k] - top)
            held = acc_out[0, rows, :] if k == 0 else acc_in[k - 1, rows, :]
            whole = whole + factor
            acc = acc + factor * held.astype(jnp.float32)
        out_ref[rows, :] = (acc / whole).astype(jnp.bfloat16)

    for copy in started:
        copy.wait_send()


def fused(
    tensor_size,
    replica_size,
    hidden,
    queries,
    stored_keys,
    stored_values,
    lengths,
    adapter_of_row,
    key_value_weight,
    adapter_down_weight,
    adapter_up_weight,
):
    T, R = tensor_size, replica_size
    step_total, row_total, feat = hidden.shape
    adapters, rank_pair, _ = adapter_down_weight.shape
    columns = adapter_up_weight.shape[2]
    tokens = step_total * row_total
    heads_here = queries.shape[2] // HEAD_SIZE
    blocks = heads_here // GROUP
    lines = tokens * heads_here
    per_row = step_total * GROUP
    span = stored_keys.shape[1]
    batch = rows_at_once(row_total, span)
    arranged = (
        queries.reshape(step_total, row_total, blocks, GROUP, HEAD_SIZE)
        .transpose(2, 1, 0, 3, 4)
        .reshape(lines, HEAD_SIZE)
    )
    bf16, f32 = jnp.bfloat16, jnp.float32
    vmem = pl.BlockSpec(memory_space=pltpu.VMEM)
    smem = pl.BlockSpec(memory_space=pltpu.SMEM)
    hbm = pl.BlockSpec(memory_space=pltpu.HBM)
    attended, fresh = pl.pallas_call(
        functools.partial(fused_kernel, T, R, row_total),
        out_shape=(
            jax.ShapeDtypeStruct((lines, HEAD_SIZE), bf16),
            jax.ShapeDtypeStruct((tokens, columns), bf16),
        ),
        in_specs=[smem, smem, hbm, vmem, hbm, hbm, hbm, hbm, hbm],
        out_specs=(vmem, vmem),
        scratch_shapes=[
            pltpu.VMEM((tokens, feat), bf16),
            pltpu.VMEM(adapter_up_weight.shape, bf16),
            pltpu.VMEM((row_total // batch, batch * per_row, batch * span), f32),
            pltpu.VMEM(stored_keys.shape, bf16),
            pltpu.VMEM(stored_values.shape, bf16),
            pltpu.VMEM((adapters * rank_pair, feat), bf16),
            pltpu.VMEM(key_value_weight.shape, bf16),
            pltpu.VMEM((T - 1, lines, HEAD_SIZE), bf16),
            pltpu.VMEM((R - 1, tokens, feat), bf16),
            pltpu.VMEM((R, row_total, 128), jnp.int32),
            pltpu.VMEM((T, tokens, columns), bf16),
            pltpu.VMEM((T - 1, tokens, columns), bf16),
            pltpu.VMEM((tokens, 128), f32),
            pltpu.VMEM((T - 1, tokens, 128), f32),
            pltpu.VMEM((adapters, rank_pair, columns), bf16),
            pltpu.VMEM((R, tokens, columns), f32),
            pltpu.VMEM((R - 1, tokens, columns), f32),
            pltpu.VMEM((T, tokens, columns), bf16),
            pltpu.VMEM((T, lines, HEAD_SIZE), bf16),
            pltpu.VMEM((T - 1, lines, HEAD_SIZE), bf16),
            pltpu.VMEM((T, 8, 128), f32),
            pltpu.VMEM((T - 1, 8, 128), f32),
            pltpu.SemaphoreType.DMA((5,)),
            pltpu.SemaphoreType.DMA((CHUNKS,)),
            pltpu.SemaphoreType.DMA((6 + 2 * blocks, T)),
            pltpu.SemaphoreType.DMA((6 + 2 * blocks, T)),
            pltpu.SemaphoreType.DMA((3, R)),
            pltpu.SemaphoreType.DMA((3, R)),
        ],
        compiler_params=pltpu.CompilerParams(
            collective_id=0, has_side_effects=True, vmem_limit_bytes=64 * 1024 * 1024
        ),
        name="fused",
    )(
        lengths,
        adapter_of_row,
        hidden.reshape(tokens, feat),
        arranged,
        adapter_up_weight,
        stored_keys,
        stored_values,
        adapter_down_weight.reshape(adapters * rank_pair, feat),
        key_value_weight,
    )
    attended = (
        attended.reshape(blocks, row_total, step_total, GROUP, HEAD_SIZE)
        .transpose(2, 1, 0, 3, 4)
        .reshape(step_total, row_total, heads_here * HEAD_SIZE)
    )
    return (attended, fresh.reshape(step_total, row_total, columns))


def fits(tensor_size, replica_size, hidden, queries, stored_keys, key_value_weight, down, up):
    heads_here = queries.shape[2] // HEAD_SIZE
    columns = up.shape[2]
    pieces = (hidden, stored_keys, stored_keys, key_value_weight, down)
    return (
        hidden.shape[0] * hidden.shape[1] == 16
        and hidden.shape[1] == 8
        and heads_here % GROUP == 0
        and columns % HEAD_SIZE == 0
        and tensor_size % 2 == 0
        and down.shape[0] * down.shape[1] == 128
        and replica_size * down.shape[1] <= 128
        and up.shape[1] % 16 == 0
        and hidden.shape[2] % (CHUNKS * 128) == 0
        and heads_here // GROUP * hidden.shape[1] * hidden.shape[0] * GROUP <= 1024
        and 256 % stored_keys.shape[1] == 0
        and sum(2 * piece.size for piece in pieces) <= 24 * 1024 * 1024
    )


def dispatch(tensor_size, replica_size, *args):
    hidden, queries, stored_keys = args[:3]
    key_value_weight, down, up = args[6:]
    if fits(tensor_size, replica_size, hidden, queries, stored_keys, key_value_weight, down, up):
        return fused(tensor_size, replica_size, *args)
    return per_device(*args)


def solution(mesh):
    placed = (
        P(None, ("groups", "replica"), "tensor"),
        P(None, ("groups", "replica"), "tensor"),
        P(("groups", "replica"), "tensor", None),
        P(("groups", "replica"), "tensor", None),
        P(("groups", "replica")),
        P(("groups", "replica")),
        P("tensor", None),
        P("replica", None, "tensor"),
        P("replica", None, "tensor"),
    )
    return jax.shard_map(
        functools.partial(dispatch, mesh.shape["tensor"], mesh.shape["replica"]),
        mesh=mesh,
        in_specs=placed,
        out_specs=(
            P(None, ("groups", "replica"), "tensor"),
            P(None, ("groups", "replica"), "tensor"),
        ),
        check_vma=False,
    )
```

```python
import functools
import math

import jax
import jax.numpy as jnp
from jax import lax
from jax.experimental import pallas as pl
from jax.experimental.pallas import tpu as pltpu
from jax.sharding import PartitionSpec as P

QUERY_HEADS = 128
KEY_VALUE_HEADS = 8
HEAD_SIZE = 128


MASKED = -1e30


def joined(value, axis, join):
    pieces = jax.tree.map(lambda part: lax.all_gather(part, axis), value)
    head = jax.tree.map(lambda part: part[0], pieces)
    tail = jax.tree.map(lambda part: part[1:], pieces)
    total, _ = lax.scan(lambda total, piece: (join(total, piece), None), head, tail)
    return total


def combine_partial(earlier, later):
    first_top, first_total, first_acc = earlier
    second_top, second_total, second_acc = later
    joined_top = jnp.maximum(first_top, second_top)
    first_factor = jnp.exp(first_top - joined_top)
    second_factor = jnp.exp(second_top - joined_top)
    joined_total = first_total * first_factor + second_total * second_factor
    joined_acc = first_acc * first_factor[..., None] + second_acc * second_factor[..., None]
    return (joined_top, joined_total, joined_acc)


def per_device(
    hidden,
    queries,
    stored_keys,
    stored_values,
    lengths,
    adapter_of_row,
    key_value_weight,
    adapter_down_weight,
    adapter_up_weight,
):
    step_total, row_total, feat_count = hidden.shape
    kv_width = key_value_weight.shape[1]
    key_value_half = kv_width // 2
    column_total = adapter_up_weight.shape[2]
    rank_width = adapter_up_weight.shape[1]
    block_count = row_total // 8
    tensor_index = lax.axis_index("tensor")
    col_start = tensor_index * column_total
    scale = 1.0 / math.sqrt(HEAD_SIZE)
    group_size = QUERY_HEADS // KEY_VALUE_HEADS
    down_all, up_part = (
        lax.all_gather(adapter_down_weight, "replica", axis=0, tiled=True),
        lax.all_gather(adapter_up_weight, "replica", axis=0, tiled=True),
    )
    block_ids = adapter_of_row.reshape(block_count, 8)[:, 0]
    down_used = jnp.take(down_all, block_ids, axis=0)
    grouped = hidden.reshape(step_total, block_count, 8, feat_count)
    low_rank = jnp.einsum("sbrd,bjd->sbrj", grouped, down_used, preferred_element_type=jnp.float32)
    base_part = jnp.dot(
        hidden.reshape(step_total * row_total, feat_count),
        key_value_weight,
        preferred_element_type=jnp.float32,
    )
    base_part = base_part.reshape(step_total, row_total, kv_width)
    up_full = lax.all_gather(up_part, "tensor", axis=2, tiled=True)
    up_used = jnp.take(up_full, block_ids, axis=0).astype(jnp.float32)
    key_delta = jnp.einsum(
        "sbri,bic->sbrc",
        low_rank[..., :rank_width],
        up_used[..., :key_value_half],
        precision=lax.Precision.HIGHEST,
    )
    value_delta = jnp.einsum(
        "sbri,bic->sbrc",
        low_rank[..., rank_width:],
        up_used[..., key_value_half:],
        precision=lax.Precision.HIGHEST,
    )
    low_delta = jnp.concatenate([key_delta, value_delta], axis=-1).reshape(
        step_total, row_total, kv_width
    )
    summed = lax.psum((base_part + low_delta).astype(jnp.bfloat16), "tensor")
    fresh_own = lax.dynamic_slice_in_dim(summed, col_start, column_total, 2)
    query_complete = lax.all_gather(queries, "tensor", axis=2, tiled=True)
    column_span = stored_keys.shape[1]
    positions = tensor_index * column_span + jnp.arange(column_span)
    usable = (positions[None, :] < lengths[:, None])[None, :, None, None, :]
    query_group_rows = query_complete.reshape(
        step_total, row_total, KEY_VALUE_HEADS, group_size, HEAD_SIZE
    )
    key_store_cache = stored_keys.reshape(row_total, column_span, KEY_VALUE_HEADS, HEAD_SIZE)
    value_store_cache = stored_values.reshape(row_total, column_span, KEY_VALUE_HEADS, HEAD_SIZE)
    scores = (
        jnp.einsum(
            "srgqd,rpgd->srgqp",
            query_group_rows,
            key_store_cache,
            preferred_element_type=jnp.float32,
        )
        * scale
    )
    scores = jnp.where(usable, scores, MASKED)
    local_top = jnp.max(scores, axis=-1)
    weights = jnp.where(usable, jnp.exp(scores - local_top[..., None]), 0.0)
    local_total = jnp.sum(weights, axis=-1).reshape(step_total, row_total, QUERY_HEADS)
    local_acc = jnp.einsum(
        "srgqp,rpgd->srgqd",
        weights.astype(jnp.bfloat16),
        value_store_cache,
        preferred_element_type=jnp.float32,
    )
    local_acc = local_acc.reshape(step_total, row_total, QUERY_HEADS, HEAD_SIZE)
    local_top = local_top.reshape(step_total, row_total, QUERY_HEADS)
    heads_here = queries.shape[2] // HEAD_SIZE
    head_start = tensor_index * heads_here
    merged_top, merged_total, merged_acc = joined(
        (local_top, local_total, local_acc), "tensor", combine_partial
    )
    row_top = lax.dynamic_slice_in_dim(merged_top, head_start, heads_here, 2)
    totals = lax.dynamic_slice_in_dim(merged_total, head_start, heads_here, 2)
    weighted = lax.dynamic_slice_in_dim(merged_acc, head_start, heads_here, 2)
    kv_of_head = (head_start + jnp.arange(heads_here)) // group_size
    newest_keys = summed[..., :key_value_half].reshape(
        step_total, row_total, KEY_VALUE_HEADS, HEAD_SIZE
    )
    newest_values = summed[..., key_value_half:].reshape(
        step_total, row_total, KEY_VALUE_HEADS, HEAD_SIZE
    )
    head_keys = jnp.take(newest_keys, kv_of_head, axis=2)
    head_values = jnp.take(newest_values, kv_of_head, axis=2)
    query_own = queries.reshape(step_total, row_total, heads_here, HEAD_SIZE)
    own_scores = (
        jnp.einsum("srhd,jrhd->srhj", query_own, head_keys, preferred_element_type=jnp.float32)
        * scale
    )
    step_index = jnp.arange(step_total)
    causal = (step_index[None, :] <= step_index[:, None])[:, None, None, :]
    own_scores = jnp.where(causal, own_scores, MASKED)
    new_top = jnp.maximum(row_top, jnp.max(own_scores, axis=-1))
    old_factor = jnp.exp(row_top - new_top)
    own_weights = jnp.where(causal, jnp.exp(own_scores - new_top[..., None]), 0.0)
    totals = totals * old_factor + jnp.sum(own_weights, axis=-1)
    own_part = jnp.einsum(
        "srhj,jrhd->srhd",
        own_weights.astype(jnp.bfloat16),
        head_values,
        preferred_element_type=jnp.float32,
    )
    weighted = weighted * old_factor[..., None] + own_part
    attended = (
        (weighted / totals[..., None])
        .astype(jnp.bfloat16)
        .reshape(step_total, row_total, heads_here * HEAD_SIZE)
    )
    return (attended, fresh_own)


MESH = pl.DeviceIdType.MESH
GROUP = QUERY_HEADS // KEY_VALUE_HEADS
CHUNKS = 8


def folded(value, width):
    shift = width
    while shift < value.shape[1]:
        value = value + pltpu.roll(value, shift, axis=1)
        shift *= 2
    return value


def fused_kernel(
    tensor_size,
    replica_size,
    row_total,
    lengths_ref,
    ids_ref,
    hidden_hbm,
    query_hbm,
    up_hbm,
    key_hbm,
    value_hbm,
    down_hbm,
    weight_hbm,
    out_ref,
    fresh_ref,
    hidden_ref,
    query_ref,
    up_ref,
    bias,
    key_buf,
    value_buf,
    down_buf,
    weight_buf,
    query_in,
    hidden_in,
    ids_in,
    base_out,
    base_in,
    low_out,
    low_in,
    up_wide,
    delta_out,
    delta_in,
    fresh_all,
    acc_out,
    acc_in,
    lse_out,
    lse_in,
    local_sem,
    weight_sem,
    t_send,
    t_recv,
    r_send,
    r_recv,
):
    T, R = tensor_size, replica_size
    t = lax.axis_index("tensor")
    r = lax.axis_index("replica")
    tokens, feat = hidden_hbm.shape
    steps = tokens // row_total
    adapters, ranks, columns = up_hbm.shape
    span = key_buf.shape[1]
    blocks = query_hbm.shape[1] // (GROUP * HEAD_SIZE)
    per_row = steps * GROUP
    per_block = row_total * per_row
    scale = 1.0 / math.sqrt(HEAD_SIZE)
    depth = feat // CHUNKS

    local = [
        pltpu.make_async_copy(down_hbm, down_buf, local_sem.at[0]),
        pltpu.make_async_copy(key_hbm, key_buf, local_sem.at[1]),
        pltpu.make_async_copy(value_hbm, value_buf, local_sem.at[2]),
    ]
    small = [
        pltpu.make_async_copy(hidden_hbm, hidden_ref, local_sem.at[3]),
        pltpu.make_async_copy(up_hbm, up_ref, local_sem.at[4]),
        pltpu.make_async_copy(query_hbm, query_ref, local_sem.at[5]),
    ]
    weights = [
        pltpu.make_async_copy(
            weight_hbm.at[pl.ds(c * depth, depth)],
            weight_buf.at[pl.ds(c * depth, depth)],
            weight_sem.at[c],
        )
        for c in range(CHUNKS)
    ]
    for copy in small[2:] + small[:2] + weights[:2] + local + weights[2:]:
        copy.start()

    def along_t(kind, k, src, dst, sign=1):
        return pltpu.make_async_remote_copy(
            src_ref=src,
            dst_ref=dst,
            send_sem=t_send.at[kind, k],
            recv_sem=t_recv.at[kind, k],
            device_id={"tensor": lax.rem(t + sign * k + T, T)},
            device_id_type=MESH,
        )

    def along_r(kind, k, src, dst):
        return pltpu.make_async_remote_copy(
            src_ref=src,
            dst_ref=dst,
            send_sem=r_send.at[kind, k],
            recv_sem=r_recv.at[kind, k],
            device_id={"replica": lax.rem(r + k, R)},
            device_id_type=MESH,
        )

    lane = lax.broadcasted_iota(jnp.int32, (row_total, 128), 1)
    sub = lax.broadcasted_iota(jnp.int32, (row_total, 128), 0)
    ids = jnp.zeros((row_total, 128), jnp.int32)
    for i in range(row_total):
        ids = jnp.where(sub == i, ids_ref[i], ids)
    ids_in[0] = ids

    barrier = pltpu.get_barrier_semaphore()
    for k in range(1, T):
        pl.semaphore_signal(
            barrier, inc=1, device_id={"tensor": lax.rem(t + k, T)}, device_id_type=MESH
        )
    for k in range(1, R):
        pl.semaphore_signal(
            barrier, inc=1, device_id={"replica": lax.rem(r + k, R)}, device_id_type=MESH
        )
    pl.semaphore_wait(barrier, T - 1 + R - 1)

    started = []

    def start(copy):
        copy.start()
        started.append(copy)
        return copy

    parts = [pl.ds(b * per_block, per_block) for b in range(blocks)]
    bands = [pl.ds(b * GROUP * HEAD_SIZE, GROUP * HEAD_SIZE) for b in range(blocks)]
    small[2].wait()
    query_moves = [
        [
            start(along_t(6 + b, k, query_ref.at[:, bands[b]], query_in.at[k - 1, :, bands[b]]))
            for k in range(1, T)
        ]
        for b in range(blocks)
    ]
    small[0].wait()
    hidden_moves = [start(along_r(0, k, hidden_ref, hidden_in.at[k - 1])) for k in range(1, R)]
    ids_moves = [start(along_r(1, k, ids_in.at[0], ids_in.at[k])) for k in range(1, R)]

    up_wide[...] = jnp.zeros_like(up_wide)
    half = (t * columns) // (T * columns // 2)
    small[1].wait()
    for a in range(adapters):
        up_wide[a, pl.ds(pl.multiple_of(half * ranks, ranks), ranks), :] = up_ref[a]

    broad = row_total * span
    line = lax.broadcasted_iota(jnp.int32, (per_block, broad), 0) % row_total
    spot = lax.broadcasted_iota(jnp.int32, (per_block, broad), 1)
    limit = jnp.zeros((1, broad), jnp.int32)
    owner_row = lax.broadcasted_iota(jnp.int32, (1, broad), 1) // span
    for i in range(row_total):
        limit = jnp.where(owner_row == i, lengths_ref[i], limit)
    bias[...] = jnp.where((line == spot // span) & (t * span + spot % span < limit), 0.0, MASKED)

    def lines_of(query, b):
        return jnp.concatenate(
            [
                query[:, h * HEAD_SIZE : (h + 1) * HEAD_SIZE]
                for h in range(b * GROUP, (b + 1) * GROUP)
            ],
            axis=0,
        )

    total = None
    for c in range(CHUNKS):
        weights[c].wait()
        part = jnp.dot(
            hidden_ref[:, c * depth : (c + 1) * depth],
            weight_buf[c * depth : (c + 1) * depth, :],
            preferred_element_type=jnp.float32,
        )
        total = part if total is None else total + part
    for u in range(T):
        base_out[u] = total[:, u * columns : (u + 1) * columns].astype(base_out.dtype)
    base_moves = [
        start(along_t(1, k, base_out.at[lax.rem(t + k, T)], base_in.at[k - 1]))
        for k in range(1, T)
    ]

    local[0].wait()
    contract = (((1,), (1,)), ((), ()))
    token_lane = lax.broadcasted_iota(jnp.int32, (tokens, 128), 1)
    pair = 2 * ranks
    low = jnp.zeros((tokens, 128), jnp.float32)
    for k in range(R):
        if k > 0:
            hidden_moves[k - 1].wait_recv()
            ids_moves[k - 1].wait_recv()
        tokens_here = hidden_ref[...] if k == 0 else hidden_in[k - 1]
        features = lax.dot_general(
            tokens_here, down_buf[...], contract, preferred_element_type=jnp.float32
        )
        mine = ids_in[k] == r * adapters + lane // pair
        features = jnp.where(jnp.concatenate([mine] * steps, axis=0), features, 0.0)
        low = jnp.where(token_lane // pair == k, folded(features, pair), low)
    low_out[...] = low
    low_moves = [start(along_t(2, k, low_out, low_in.at[k - 1])) for k in range(1, T)]

    local[1].wait()
    local[2].wait()
    lse_lane = lax.broadcasted_iota(jnp.int32, (per_row, 128), 1)
    count = blocks * row_total

    def attend(owner, query, slot, b, lse):
        cols = pl.ds(pl.multiple_of((owner * blocks + b) * HEAD_SIZE, HEAD_SIZE), HEAD_SIZE)
        scores = bias[...] + scale * lax.dot_general(
            lines_of(query, b),
            key_buf[:, :, cols].reshape(broad, HEAD_SIZE),
            contract,
            preferred_element_type=jnp.float32,
        )
        top = jnp.max(scores, axis=1, keepdims=True)
        wide = jnp.exp(scores - top)
        whole = jnp.sum(wide, axis=1, keepdims=True)
        acc = jnp.dot(
            wide.astype(jnp.bfloat16),
            value_buf[:, :, cols].reshape(broad, HEAD_SIZE),
            preferred_element_type=jnp.float32,
        )
        acc_out[slot, b * per_block : (b + 1) * per_block, :] = (acc * (1.0 / whole)).astype(
            jnp.bfloat16
        )
        level = top + jnp.log(whole)
        for i in range(row_total):
            piece = level[i * per_row : (i + 1) * per_row]
            lse = jnp.where(lse_lane == b * row_total + i, piece, lse)
        return lse

    def pack(lse, slot):
        slab = lse[:8]
        for v in range(1, per_row // 8):
            moved = pltpu.roll(lse[8 * v : 8 * v + 8], v * count, axis=1)
            slab = jnp.where(lane // count == v, moved, slab)
        lse_out[slot] = slab

    levels_of = [jnp.full((per_row, 128), MASKED, jnp.float32)] * T
    acc_moves, lse_moves = [[] for _ in range(blocks)], []

    def attend_remote(b):
        for k in range(1, T):
            query_moves[b][k - 1].wait_recv()
            owner = lax.rem(t - k + T, T)
            levels_of[k] = attend(owner, query_in.at[k - 1], k, b, levels_of[k])
            source, target = acc_out.at[k, parts[b]], acc_in.at[k - 1, parts[b]]
            acc_moves[b].append(start(along_t(6 + blocks + b, k, source, target, -1)))
            if b == blocks - 1:
                pack(levels_of[k], k)
                lse_moves.append(start(along_t(4, k, lse_out.at[k], lse_in.at[k - 1], -1)))

    for b in range(blocks - 1):
        attend_remote(b)

    for move in low_moves:
        move.wait_recv()
    packed = low_out[...]
    for j in range(T - 1):
        packed = packed + low_in[j]
    wide_up = up_wide[...].reshape(adapters * 2 * ranks, columns)
    for k in range(R):
        low = folded(jnp.where(token_lane // pair == k, packed, 0.0), pair)
        mine = ids_in[k] == r * adapters + lane // pair
        low = jnp.where(jnp.concatenate([mine] * steps, axis=0), low, 0.0)
        high = low.astype(jnp.bfloat16)
        rest = (low - high.astype(jnp.float32)).astype(jnp.bfloat16)
        delta_out[k] = jnp.dot(high, wide_up, preferred_element_type=jnp.float32) + jnp.dot(
            rest, wide_up, preferred_element_type=jnp.float32
        )
    delta_moves = []
    for k in range(1, R):
        delta_moves.append(
            start(
                pltpu.make_async_remote_copy(
                    src_ref=delta_out.at[k],
                    dst_ref=delta_in.at[k - 1],
                    send_sem=r_send.at[2, k],
                    recv_sem=r_recv.at[2, k],
                    device_id={"replica": lax.rem(r - k + R, R)},
                    device_id_type=MESH,
                )
            )
        )

    attend_remote(blocks - 1)

    fresh = base_out[t].astype(jnp.float32) + delta_out[0]
    for move in base_moves:
        move.wait_recv()
    for k in range(1, T):
        fresh = fresh + base_in[k - 1].astype(jnp.float32)
    for move in delta_moves:
        move.wait_recv()
    for k in range(1, R):
        fresh = fresh + delta_in[k - 1]
    fresh = fresh.astype(jnp.bfloat16)
    fresh_ref[...] = fresh
    fresh_all[t] = fresh
    fresh_moves = [
        start(along_t(5, k, fresh_all.at[t], fresh_all.at[t])) for k in range(1, T)
    ]
    for b in range(blocks):
        levels_of[0] = attend(t, query_ref, 0, b, levels_of[0])
    pack(levels_of[0], 0)

    for move in fresh_moves + lse_moves:
        move.wait_recv()

    line = lax.broadcasted_iota(jnp.int32, (per_block, tokens), 0)
    spot = lax.broadcasted_iota(jnp.int32, (per_block, tokens), 1)
    token = line % tokens
    seen = (token % row_total == spot % row_total) & (spot // row_total <= token // row_total)
    for b in range(blocks):
        for move in acc_moves[b]:
            move.wait_recv()
        column = (t * blocks + b) * HEAD_SIZE
        holder, offset = column // columns, lax.rem(column, columns)
        cols = pl.ds(pl.multiple_of(offset, HEAD_SIZE), HEAD_SIZE)
        new_keys = fresh_all[holder, :, cols]
        new_values = fresh_all[T // 2 + holder, :, cols]
        rows = slice(b * per_block, (b + 1) * per_block)
        scores = scale * lax.dot_general(
            lines_of(query_ref, b), new_keys, contract, preferred_element_type=jnp.float32
        )
        scores = jnp.where(seen, scores, MASKED)
        top = jnp.max(scores, axis=1, keepdims=True)
        levels = []
        for k in range(T):
            held = lse_out[0] if k == 0 else lse_in[k - 1]
            levels.append(
                jnp.concatenate(
                    [
                        held[:, v * count + b * row_total + i : v * count + b * row_total + i + 1]
                        for i in range(row_total)
                        for v in range(per_row // 8)
                    ],
                    axis=0,
                )
            )
            top = jnp.maximum(top, levels[-1])
        wide = jnp.where(seen, jnp.exp(scores - top), 0.0)
        whole = jnp.sum(wide, axis=1, keepdims=True)
        acc = jnp.dot(wide.astype(jnp.bfloat16), new_values, preferred_element_type=jnp.float32)
        for k in range(T):
            factor = jnp.exp(levels[k] - top)
            held = acc_out[0, rows, :] if k == 0 else acc_in[k - 1, rows, :]
            whole = whole + factor
            acc = acc + factor * held.astype(jnp.float32)
        done = (acc / whole).astype(jnp.bfloat16)
        for g in range(GROUP):
            head = b * GROUP + g
            out_ref[:, head * HEAD_SIZE : (head + 1) * HEAD_SIZE] = done[
                g * tokens : (g + 1) * tokens
            ]

    for copy in started:
        copy.wait_send()


def fused(
    tensor_size,
    replica_size,
    hidden,
    queries,
    stored_keys,
    stored_values,
    lengths,
    adapter_of_row,
    key_value_weight,
    adapter_down_weight,
    adapter_up_weight,
):
    T, R = tensor_size, replica_size
    step_total, row_total, feat = hidden.shape
    adapters, rank_pair, _ = adapter_down_weight.shape
    columns = adapter_up_weight.shape[2]
    tokens = step_total * row_total
    heads_here = queries.shape[2] // HEAD_SIZE
    blocks = heads_here // GROUP
    lines = tokens * heads_here
    per_row = step_total * GROUP
    span = stored_keys.shape[1]
    bf16, f32 = jnp.bfloat16, jnp.float32
    vmem = pl.BlockSpec(memory_space=pltpu.VMEM)
    smem = pl.BlockSpec(memory_space=pltpu.SMEM)
    hbm = pl.BlockSpec(memory_space=pltpu.HBM)
    attended, fresh = pl.pallas_call(
        functools.partial(fused_kernel, T, R, row_total),
        out_shape=(
            jax.ShapeDtypeStruct((tokens, queries.shape[2]), bf16),
            jax.ShapeDtypeStruct((tokens, columns), bf16),
        ),
        in_specs=[smem, smem, hbm, hbm, hbm, hbm, hbm, hbm, hbm],
        out_specs=(vmem, vmem),
        scratch_shapes=[
            pltpu.VMEM((tokens, feat), bf16),
            pltpu.VMEM((tokens, queries.shape[2]), bf16),
            pltpu.VMEM(adapter_up_weight.shape, bf16),
            pltpu.VMEM((row_total * per_row, row_total * span), f32),
            pltpu.VMEM(stored_keys.shape, bf16),
            pltpu.VMEM(stored_values.shape, bf16),
            pltpu.VMEM((adapters * rank_pair, feat), bf16),
            pltpu.VMEM(key_value_weight.shape, bf16),
            pltpu.VMEM((T - 1, tokens, queries.shape[2]), bf16),
            pltpu.VMEM((R - 1, tokens, feat), bf16),
            pltpu.VMEM((R, row_total, 128), jnp.int32),
            pltpu.VMEM((T, tokens, columns), bf16),
            pltpu.VMEM((T - 1, tokens, columns), bf16),
            pltpu.VMEM((tokens, 128), f32),
            pltpu.VMEM((T - 1, tokens, 128), f32),
            pltpu.VMEM((adapters, rank_pair, columns), bf16),
            pltpu.VMEM((R, tokens, columns), f32),
            pltpu.VMEM((R - 1, tokens, columns), f32),
            pltpu.VMEM((T, tokens, columns), bf16),
            pltpu.VMEM((T, lines, HEAD_SIZE), bf16),
            pltpu.VMEM((T - 1, lines, HEAD_SIZE), bf16),
            pltpu.VMEM((T, 8, 128), f32),
            pltpu.VMEM((T - 1, 8, 128), f32),
            pltpu.SemaphoreType.DMA((6,)),
            pltpu.SemaphoreType.DMA((CHUNKS,)),
            pltpu.SemaphoreType.DMA((6 + 2 * blocks, T)),
            pltpu.SemaphoreType.DMA((6 + 2 * blocks, T)),
            pltpu.SemaphoreType.DMA((3, R)),
            pltpu.SemaphoreType.DMA((3, R)),
        ],
        compiler_params=pltpu.CompilerParams(
            collective_id=0, has_side_effects=True, vmem_limit_bytes=64 * 1024 * 1024
        ),
        name="fused",
    )(
        lengths,
        adapter_of_row,
        hidden.reshape(tokens, feat),
        queries.reshape(tokens, queries.shape[2]),
        adapter_up_weight,
        stored_keys,
        stored_values,
        adapter_down_weight.reshape(adapters * rank_pair, feat),
        key_value_weight,
    )
    attended = attended.reshape(queries.shape)
    return (attended, fresh.reshape(step_total, row_total, columns))


def fits(tensor_size, replica_size, hidden, queries, stored_keys, key_value_weight, down, up):
    heads_here = queries.shape[2] // HEAD_SIZE
    columns = up.shape[2]
    pieces = (hidden, stored_keys, stored_keys, key_value_weight, down)
    return (
        hidden.shape[0] * hidden.shape[1] == 16
        and hidden.shape[1] == 8
        and heads_here % GROUP == 0
        and columns % HEAD_SIZE == 0
        and tensor_size % 2 == 0
        and down.shape[0] * down.shape[1] == 128
        and replica_size * down.shape[1] <= 128
        and up.shape[1] % 16 == 0
        and hidden.shape[2] % (CHUNKS * 128) == 0
        and heads_here // GROUP * hidden.shape[1] * hidden.shape[0] * GROUP <= 1024
        and 256 % stored_keys.shape[1] == 0
        and sum(2 * piece.size for piece in pieces) <= 24 * 1024 * 1024
    )


def dispatch(tensor_size, replica_size, *args):
    hidden, queries, stored_keys = args[:3]
    key_value_weight, down, up = args[6:]
    if fits(tensor_size, replica_size, hidden, queries, stored_keys, key_value_weight, down, up):
        return fused(tensor_size, replica_size, *args)
    return per_device(*args)


def solution(mesh):
    placed = (
        P(None, ("groups", "replica"), "tensor"),
        P(None, ("groups", "replica"), "tensor"),
        P(("groups", "replica"), "tensor", None),
        P(("groups", "replica"), "tensor", None),
        P(("groups", "replica")),
        P(("groups", "replica")),
        P("tensor", None),
        P("replica", None, "tensor"),
        P("replica", None, "tensor"),
    )
    return jax.shard_map(
        functools.partial(dispatch, mesh.shape["tensor"], mesh.shape["replica"]),
        mesh=mesh,
        in_specs=placed,
        out_specs=(
            P(None, ("groups", "replica"), "tensor"),
            P(None, ("groups", "replica"), "tensor"),
        ),
        check_vma=False,
    )
```
